32 devices in a mesh: slab: 8 (over z, x), grp: 4 (over y, core).
Axes of the slice: x: 2, y: 2, z: 4, core: 2. Of those that a mesh axis runs over, the one named last changes fastest.
Arguments:
- volume: bfloat16 [8, 32, 64, 1024], P('slab', 'grp'), may hold values from -6 to 6
- vis_mask: int32 [8, 32, 64], P('slab', 'grp'), may hold values from 0 to 1, as said below
- enc_gain: bfloat16 [1024], replicated, may hold values from 0.099609375 to 1.8984375
- enc_wqk: bfloat16 [1024, 2048], replicated
- enc_wv: bfloat16 [1024, 1024], replicated, may hold values from -0.1875 to 0.1875
- enc_wo: bfloat16 [1024, 1024], replicated, may hold values from -0.1875 to 0.1875
- final_gain: bfloat16 [1024], replicated, may hold values from 0.099609375 to 1.8984375
- embed_w: bfloat16 [1024, 512], replicated, may hold values from -0.1875 to 0.1875
- mask_token: bfloat16 [512], replicated, may hold values from -4 to 4
- depth_pos: bfloat16 [8, 512], replicated, may hold values from -3 to 3
- row_pos: bfloat16 [32, 512], replicated, may hold values from -3 to 3
- col_pos: bfloat16 [64, 512], replicated, may hold values from -3 to 3
- dec_gain: bfloat16 [512], replicated, may hold values from 0.099609375 to 1.8984375
- dec_wqk: bfloat16 [512, 1024], replicated
- dec_wv: bfloat16 [512, 512], replicated, may hold values from -0.25 to 0.25
- dec_wo: bfloat16 [512, 512], replicated, may hold values from -0.25 to 0.25
Outputs:
- decoded: bfloat16 [8, 32, 64, 512], P('slab', 'grp')
The draws below stay inside these ranges and needn't reach their ends.
Inputs may be any that keep to these rules, and one draw needn't show every extreme that they name: `vis_mask`: in each block of 8 consecutive depth slices (starting at a multiple of 8) and the 8 plane rows of one grp index, exactly 1024 tokens are visible. The 512 tokens of one depth slice in such a block hold 64 to 192 visible ones, and 192 is reached in every block.
All inputs are finite; a program needn't handle non-finite values.
Results may differ from the reference program's by a relative error of at most 0.0098.
Values may be sent and summed in bfloat16 or wider, within the bound.
A program may use at most 128 MiB of HBM per device.

```python
import jax
import jax.numpy as jnp
from jax import lax

D = 1024
HEADS = 16
DD = 512
DHEADS = 16
WIN_SLABS = 8
NW = 64
H_DEV = 8
VIS_DEV = 128
NZ = 8
NH = 32


def query_key_pair(key, salt, width):
    base_key = jax.random.fold_in(key, salt)
    key_query, key_noise = jax.random.split(base_key, 2)
    spread_scale = (3.0 / width) ** 0.5
    query_part = jax.random.normal(key_query, (width, width), jnp.float32) * spread_scale
    noise_part = jax.random.normal(key_noise, (width, width), jnp.float32) * spread_scale
    key_part = noise_part
    return jnp.concatenate([query_part, key_part], axis=1)


def draw_enc_wqk(key, part):
    return query_key_pair(key, 101, D).astype(jnp.bfloat16)


def draw_dec_wqk(key, part):
    return query_key_pair(key, 202, DD).astype(jnp.bfloat16)


def draw_vis_mask(key, part):
    blocks_depth = NZ // WIN_SLABS
    blocks_row = NH // H_DEV
    block_total = blocks_depth * blocks_row
    tokens_dev = H_DEV * NW
    key_order, key_delta, key_token = jax.random.split(jax.random.fold_in(key, 7), 3)
    raw_scores = jax.random.randint(key_order, (block_total, WIN_SLABS), 0, 1 << 20) * WIN_SLABS
    raw_scores = raw_scores + jnp.arange(WIN_SLABS, dtype=jnp.int32)[None, :]
    slab_order = jnp.argsort(raw_scores, axis=1).astype(jnp.int32)
    spreads = jax.random.randint(key_delta, (block_total, WIN_SLABS // 2 - 1), 0, VIS_DEV * 3 // 8 + 1)
    largest = jnp.full((block_total, 1), VIS_DEV // 2, jnp.int32)
    halves = jnp.concatenate([largest, spreads.astype(jnp.int32)], axis=1)
    deltas = jnp.stack([halves, -halves], axis=2).reshape(block_total, WIN_SLABS)
    one_hot = (slab_order[:, :, None] == jnp.arange(WIN_SLABS, dtype=jnp.int32)[None, None, :]).astype(jnp.int32)
    counts = VIS_DEV + jnp.sum(deltas[:, :, None] * one_hot, axis=1)
    counts = counts.reshape(blocks_depth, blocks_row, WIN_SLABS).transpose(0, 2, 1).reshape(NZ, blocks_row, 1)
    token_scores = jax.random.randint(key_token, (NZ, blocks_row, tokens_dev), 0, 1 << 20) * tokens_dev
    token_scores = token_scores + jnp.arange(tokens_dev, dtype=jnp.int32)[None, None, :]
    ranks = jnp.argsort(jnp.argsort(token_scores, axis=2), axis=2).astype(jnp.int32)
    visible = (ranks < counts).astype(jnp.int32)
    return visible.reshape(NZ, blocks_row, H_DEV, NW).reshape(NZ, NH, NW)


def levels(own_key, extent, cuts, smallest, top_value):
    def one(position, shards_of):
        steps = jax.random.uniform(jax.random.fold_in(jax.random.fold_in(own_key, 6), position), (shards_of,), jnp.float32, smallest / len(cuts), top_value / len(cuts))
        return jnp.repeat(jnp.exp(steps), extent[position] // shards_of).reshape((-1,) + (1,) * (len(extent) - position - 1))

    level = one(*cuts[0])
    for cut in cuts[1:]:
        level = level * one(*cut)
    return level


def gaussian(key, shape, spread, bound, cuts=(), kind=jnp.bfloat16):
    drawn = jax.random.normal(key, shape, jnp.float32) * spread
    if len(cuts) > 0:
        drawn = levels(key, shape, cuts, -0.22, 0.18) * drawn
    return jnp.clip(drawn, min=-bound, max=bound).astype(kind)


def setup_inputs(seed: int = 0) -> dict:
    key_of = jax.random.split(jax.random.key(seed), 17)
    return {
        "volume": gaussian(key_of[0], (NZ, NH, NW, D), 1.0, 6.0, ((0, 8), (1, 4))),
        "vis_mask": draw_vis_mask(jax.random.fold_in(key_of[16], 71), 0),
        "enc_gain": jnp.clip(1.0 + 0.18 * jax.random.normal(key_of[2], (D,), jnp.float32), 0.099609375, 1.8984375).astype(jnp.bfloat16),
        "enc_wqk": draw_enc_wqk(jax.random.fold_in(key_of[16], 71), 0),
        "enc_wv": gaussian(key_of[4], (D, D), D ** -0.5, 0.1875),
        "enc_wo": gaussian(key_of[5], (D, D), D ** -0.5, 0.1875),
        "final_gain": jnp.clip(1.0 + 0.18 * jax.random.normal(key_of[6], (D,), jnp.float32), 0.099609375, 1.8984375).astype(jnp.bfloat16),
        "embed_w": gaussian(key_of[7], (D, DD), D ** -0.5, 0.1875),
        "mask_token": gaussian(key_of[8], (DD,), 1.0, 4.0),
        "depth_pos": gaussian(key_of[9], (NZ, DD), 0.5, 3.0),
        "row_pos": gaussian(key_of[10], (NH, DD), 0.5, 3.0),
        "col_pos": gaussian(key_of[11], (NW, DD), 0.5, 3.0),
        "dec_gain": jnp.clip(1.0 + 0.18 * jax.random.normal(key_of[12], (DD,), jnp.float32), 0.099609375, 1.8984375).astype(jnp.bfloat16),
        "dec_wqk": draw_dec_wqk(jax.random.fold_in(key_of[16], 71), 0),
        "dec_wv": gaussian(key_of[14], (DD, DD), DD ** -0.5, 0.25),
        "dec_wo": gaussian(key_of[15], (DD, DD), DD ** -0.5, 0.25),
    }


def layer_norm(values, gain):
    values = values.astype(jnp.float32)
    average = lax.optimization_barrier(jnp.mean(values, axis=-1, keepdims=True))
    centered = values - average
    variance = lax.optimization_barrier(jnp.mean(centered * centered, axis=-1, keepdims=True))
    return centered * lax.rsqrt(variance + 1e-05) * gain.astype(jnp.float32)

def softmax_rows(scores):
    row_max = lax.optimization_barrier(jnp.max(scores, axis=-1, keepdims=True))
    exponent = jnp.exp(scores - row_max)
    return (exponent / lax.optimization_barrier(jnp.sum(exponent, axis=-1, keepdims=True))).astype(jnp.bfloat16)

def encode_rows(row_data, enc_gain, enc_wqk, enc_wv, enc_wo, final_gain, embed_w):
    width = row_data.shape[1]
    head_size = width // HEADS
    normed = layer_norm(row_data, enc_gain).astype(jnp.bfloat16)
    query_key = jnp.dot(normed, enc_wqk, preferred_element_type=jnp.float32).astype(jnp.bfloat16)
    queries = query_key[:, :width]
    key_rows = query_key[:, width:]
    value_rows = jnp.dot(normed, enc_wv, preferred_element_type=jnp.float32).astype(jnp.bfloat16)
    score_scale = head_size ** (-0.5)

    def head_context(head_index):
        offset = head_index * head_size
        query_part = lax.dynamic_slice_in_dim(queries, offset, head_size, 1)
        key_part = lax.dynamic_slice_in_dim(key_rows, offset, head_size, 1)
        value_part = lax.dynamic_slice_in_dim(value_rows, offset, head_size, 1)
        scores = jnp.dot(query_part, key_part.T, preferred_element_type=jnp.float32) * score_scale
        return jnp.dot(softmax_rows(scores), value_part, preferred_element_type=jnp.float32).astype(jnp.bfloat16)
    context = lax.map(head_context, jnp.arange(HEADS, dtype=jnp.int32))
    context = jnp.transpose(context, (1, 0, 2)).reshape(row_data.shape[0], width)
    mixed = row_data.astype(jnp.float32) + jnp.dot(context, enc_wo, preferred_element_type=jnp.float32)
    encoded = layer_norm(mixed, final_gain).astype(jnp.bfloat16)
    return jnp.dot(encoded, embed_w, preferred_element_type=jnp.float32).astype(jnp.bfloat16)

def decode_rows(block, dec_gain, dec_wqk, dec_wv, dec_wo):
    depth, count, width = block.shape
    head_size = width // DHEADS
    normed = layer_norm(block, dec_gain).astype(jnp.bfloat16).reshape(depth * count, width)
    query_key = jnp.dot(normed, dec_wqk, preferred_element_type=jnp.float32).astype(jnp.bfloat16)
    value_rows = jnp.dot(normed, dec_wv, preferred_element_type=jnp.float32).astype(jnp.bfloat16)
    queries = query_key[:, :width].reshape(depth, count, DHEADS, head_size)
    key_rows = query_key[:, width:].reshape(depth, count, DHEADS, head_size)
    value_rows = value_rows.reshape(depth, count, DHEADS, head_size)
    scores = jnp.einsum('zphd,yphd->phzy', queries.astype(jnp.float32), key_rows.astype(jnp.float32)) * head_size ** (-0.5)
    probs = softmax_rows(scores)
    context = jnp.einsum('phzy,yphd->zphd', probs.astype(jnp.float32), value_rows.astype(jnp.float32))
    context = context.astype(jnp.bfloat16).reshape(depth * count, width)
    mixed = block.reshape(depth * count, width).astype(jnp.float32) + jnp.dot(context, dec_wo, preferred_element_type=jnp.float32)
    return mixed.astype(jnp.bfloat16).reshape(depth, count, width)

def reference(volume, vis_mask, enc_gain, enc_wqk, enc_wv, enc_wo, final_gain, embed_w, mask_token, depth_pos, row_pos, col_pos, dec_gain, dec_wqk, dec_wv, dec_wo):
    window_count = NZ // WIN_SLABS
    window_tokens = WIN_SLABS * NH * NW
    window_visible = WIN_SLABS * (NH // H_DEV) * VIS_DEV
    volume_windows = volume.reshape(window_count, window_tokens, D)
    mask_windows = vis_mask.reshape(window_count, window_tokens)

    def encode_window(pair):
        window_rows, window_mask = pair
        row_order = jnp.argsort(1 - window_mask, stable=True)[:window_visible]
        embedded = encode_rows(window_rows[row_order], enc_gain, enc_wqk, enc_wv, enc_wo, final_gain, embed_w)
        filled = jnp.broadcast_to(mask_token[None, :], (window_tokens, DD))
        return filled.at[row_order].set(embedded)
    tokens_in = lax.map(encode_window, (volume_windows, mask_windows)).reshape(NZ, NH, NW, DD)
    streams = tokens_in.astype(jnp.float32) + depth_pos.astype(jnp.float32)[:, None, None, :]
    streams = streams + row_pos.astype(jnp.float32)[None, :, None, :]
    streams = streams + col_pos.astype(jnp.float32)[None, None, :, :]
    streams = streams.astype(jnp.bfloat16)

    def decode_plane_row(block):
        return decode_rows(block, dec_gain, dec_wqk, dec_wv, dec_wo)
    decoded = lax.map(decode_plane_row, jnp.moveaxis(streams, 1, 0))
    return jnp.moveaxis(decoded, 0, 1)
```

```python
import functools

import jax
import jax.numpy as jnp
from jax import lax
from jax.experimental import pallas as pl
from jax.experimental.pallas import tpu as pltpu
from jax.sharding import Mesh, PartitionSpec as P

HEADS = 16
DHEADS = 16
WIN_SLABS = 8
MOST = 192
HALF = MOST // 2
COUNT_ROWS = 16
KV_ROWS = MOST + COUNT_ROWS
SEND_ROWS = KV_ROWS + HALF
QUAD = 4
LOG2E = 1.4426950408889634
F32 = jnp.float32
BF16 = jnp.bfloat16


def dot(a, b):
    return lax.dot_general(a, b, (((1,), (0,)), ((), ())), preferred_element_type=F32)


def dot_nt(a, b):
    return lax.dot_general(a, b, (((1,), (1,)), ((), ())), preferred_element_type=F32)


def norm(values, gain):
    average = jnp.mean(values, axis=-1, keepdims=True)
    centered = values - average
    variance = jnp.mean(centered * centered, axis=-1, keepdims=True)
    return centered * lax.rsqrt(variance + 1e-05) * gain.astype(F32)


def iota(shape, dim):
    return lax.broadcasted_iota(jnp.int32, shape, dim)


def project_kernel(mask, volume, gain, wq, wk, wv, sent, rows, normed):
    tokens = volume.shape[0]

    @pl.when(pl.program_id(0) == 0)
    def _():
        seen = mask[...] == 1
        seen_rows = jnp.broadcast_to(jnp.where(seen, 1.0, 0.0), (16, tokens)).astype(BF16)
        upper = jnp.where(iota((tokens, tokens), 0) <= iota((tokens, tokens), 1), 1.0, 0.0)
        rank = dot(seen_rows, upper.astype(BF16))[0:1, :].astype(jnp.int32) - 1
        rank = jnp.where(seen, rank, -1)
        pick = jnp.where(iota((MOST, tokens), 0) == rank, 1.0, 0.0).astype(BF16)
        row_data = dot(pick, volume[...])
        rows[...] = row_data.astype(BF16)
        normed[...] = norm(row_data, gain[...]).astype(BF16)

    count = jnp.sum(jnp.where(mask[...] == 1, 1.0, 0.0), axis=1, keepdims=True)
    x = normed[...]
    size = wq.shape[1] // QUAD
    q = dot(x, wq[...]) * (size ** (-0.5) * LOG2E)
    k = dot(x, wk[...])
    v = dot(x, wv[...])
    for i in range(QUAD):
        part = slice(i * size, (i + 1) * size)
        sent[i, 0:MOST, :] = jnp.concatenate([k[:, part], v[:, part]], axis=1).astype(BF16)
        sent[i, MOST:KV_ROWS, :] = jnp.broadcast_to(count, (COUNT_ROWS, 2 * size)).astype(BF16)
        sent[i, KV_ROWS:SEND_ROWS, :] = jnp.concatenate(
            [q[0:HALF, part], q[HALF:MOST, part]], axis=1
        ).astype(BF16)


def project(mask, volume, gain, wqk, wv):
    tokens, width = volume.shape
    steps = HEADS // QUAD
    cols = width // steps
    lanes = 2 * (width // HEADS)
    return pl.pallas_call(
        project_kernel,
        grid=(steps,),
        in_specs=[
            pl.BlockSpec((1, tokens), lambda j: (0, 0)),
            pl.BlockSpec((tokens, width), lambda j: (0, 0)),
            pl.BlockSpec((1, width), lambda j: (0, 0)),
            pl.BlockSpec((width, cols), lambda j: (0, j)),
            pl.BlockSpec((width, cols), lambda j: (0, j + steps)),
            pl.BlockSpec((width, cols), lambda j: (0, j)),
        ],
        out_specs=[
            pl.BlockSpec((QUAD, SEND_ROWS, lanes), lambda j: (j, 0, 0)),
            pl.BlockSpec((MOST, width), lambda j: (0, 0)),
        ],
        out_shape=[
            jax.ShapeDtypeStruct((HEADS, SEND_ROWS, lanes), BF16),
            jax.ShapeDtypeStruct((MOST, width), BF16),
        ],
        scratch_shapes=[pltpu.VMEM((MOST, width), BF16)],
        compiler_params=pltpu.CompilerParams(vmem_limit_bytes=40 << 20),
        name="project",
    )(mask, volume, gain, wqk, wqk, wv)


TILE = 256


def attend_kernel(counts, mine, other, out, packed, queries, keys, values, results):
    blocks = mine.shape[0]
    lanes = mine.shape[2]
    size = lanes // 2
    total = keys.shape[0]
    half = total // 2
    zero = jnp.zeros((MOST, size), F32)
    offset = 0
    starts = []
    for i in range(2 * blocks):
        source = mine if i < blocks else other
        packed[pl.ds(offset, MOST), :] = source[i % blocks, 0:MOST, :].astype(F32)
        if i < blocks:
            starts.append(offset)
        offset = offset + counts[i]
    for i in range(0, total, TILE):
        both = packed[i : i + TILE, :]
        keys[i : i + TILE, :] = both.astype(BF16)
        values[i : i + TILE, :] = jnp.where(iota((TILE, lanes), 1) < size, 1.0, both).astype(BF16)
    for i in range(blocks):
        q = mine[i, KV_ROWS:SEND_ROWS, :].astype(F32)
        q = jnp.concatenate([q[:, :size], q[:, size:]], axis=0)
        packed[pl.ds(starts[i], MOST), :] = jnp.concatenate([q, zero], axis=1)
    for i in range(0, half, TILE):
        queries[i : i + TILE, :] = packed[i : i + TILE, :].astype(BF16)
    results[half:, :] = jnp.zeros((results.shape[0] - half, lanes), F32)

    def step(t, carry):
        at = pl.multiple_of(t * TILE, TILE)
        scores = dot_nt(queries[pl.ds(at, TILE), :], keys[...])
        top = jnp.max(scores, axis=-1, keepdims=True)
        weight = jnp.exp2(scores - top).astype(BF16)
        mixed = dot(weight, values[...])
        results[pl.ds(at, TILE), :] = mixed / pltpu.roll(mixed, size, 1)
        return carry

    lax.fori_loop(0, half // TILE, step, 0)
    for i in range(blocks):
        block = results[pl.ds(starts[i], MOST), :][:, size:]
        out[i, :, :] = jnp.concatenate([block[0:HALF], block[HALF:MOST]], axis=1).astype(BF16)


def attend(counts, mine, other, total):
    blocks, _, lanes = mine.shape
    whole = pl.BlockSpec(memory_space=pltpu.VMEM)
    return pl.pallas_call(
        attend_kernel,
        in_specs=[pl.BlockSpec(memory_space=pltpu.SMEM), whole, whole],
        out_specs=whole,
        out_shape=jax.ShapeDtypeStruct((blocks, HALF, lanes), BF16),
        scratch_shapes=[
            pltpu.VMEM((total + MOST, lanes), F32),
            pltpu.VMEM((total // 2, lanes), BF16),
            pltpu.VMEM((total, lanes), BF16),
            pltpu.VMEM((total, lanes), BF16),
            pltpu.VMEM((total // 2 + MOST, lanes), F32),
        ],
        compiler_params=pltpu.CompilerParams(vmem_limit_bytes=48 << 20),
        name="attend",
    )(counts, mine, other)


def merge_kernel(
    plane_rows, mask, rows, context, wo, gain, embed, mask_token, depth_pos, row_pos, col_pos, out
):
    tokens = out.shape[0]
    plane_cols = tokens // plane_rows
    heads, _, lanes = context.shape
    size = lanes // 2
    tiles = []
    for j in range(0, heads, 2):
        a, b = context[j], context[j + 1]
        tiles.append(
            jnp.concatenate(
                [
                    jnp.concatenate([a[:, :size], b[:, :size]], axis=1),
                    jnp.concatenate([a[:, size:], b[:, size:]], axis=1),
                ],
                axis=0,
            )
        )
    mixed = rows[...].astype(F32) + dot(jnp.concatenate(tiles, axis=1), wo[...])
    encoded = norm(mixed, gain[...]).astype(BF16)
    embedded = dot(encoded, embed[...]).astype(BF16)

    seen = jnp.broadcast_to(jnp.where(mask[...] == 1, 1.0, 0.0), (16, tokens)).astype(BF16)
    down, across = iota((tokens, tokens), 0), iota((tokens, tokens), 1)
    rank = dot_nt(jnp.where(across <= down, 1.0, 0.0).astype(BF16), seen)[:, 0:1]
    shown = dot_nt(jnp.where(across == down, 1.0, 0.0).astype(BF16), seen)[:, 0:1] > 0.5
    rank = jnp.where(shown, rank.astype(jnp.int32) - 1, -1)
    place = jnp.where(iota((tokens, MOST), 1) == rank, 1.0, 0.0).astype(BF16)
    stream = dot(place, embedded)
    stream = jnp.where(shown, stream, mask_token[...].astype(F32))

    depth = lax.axis_index("win") * lax.axis_size("slab") + lax.axis_index("slab")
    grp = lax.axis_index("y") * lax.axis_size("half") + lax.axis_index("half")
    depths = depth_pos[...].astype(F32)
    chosen = jnp.where(iota(depths.shape, 0) == depth, depths, 0.0)
    stream = stream + jnp.sum(chosen, axis=0, keepdims=True)
    row_count, col_count = row_pos.shape[0], col_pos.shape[0]
    row = iota((tokens, row_count), 0) // plane_cols + grp * plane_rows
    row_hot = jnp.where(iota((tokens, row_count), 1) == row, 1.0, 0.0).astype(BF16)
    stream = stream + dot(row_hot, row_pos[...])
    col = iota((tokens, col_count), 0) % plane_cols
    col_hot = jnp.where(iota((tokens, col_count), 1) == col, 1.0, 0.0).astype(BF16)
    stream = stream + dot(col_hot, col_pos[...])
    out[...] = stream.astype(BF16)


def merge(plane_rows, mask, rows, context, wo, gain, embed, mask_token, *positions):
    tokens = mask.shape[1]
    whole = pl.BlockSpec(memory_space=pltpu.VMEM)
    return pl.pallas_call(
        functools.partial(merge_kernel, plane_rows),
        in_specs=[whole] * 10,
        out_specs=whole,
        out_shape=jax.ShapeDtypeStruct((tokens, embed.shape[1]), BF16),
        compiler_params=pltpu.CompilerParams(vmem_limit_bytes=40 << 20),
        name="merge",
    )(mask, rows, context, wo, gain, embed, mask_token, *positions)


def decode_kernel(depth, block, gain, wqk, wv, wo, out, queries, keys, values, context):
    tokens, width = block.shape
    spots = tokens // depth
    size = width // DHEADS
    x = block[...].astype(F32)
    normed = norm(x, gain[...]).astype(BF16)
    queries[...] = dot(normed, wqk[:, :width]).astype(BF16).astype(F32)
    keys[...] = dot(normed, wqk[:, width:]).astype(BF16).astype(F32)
    values[...] = dot(normed, wv[...]).astype(BF16).astype(F32)
    lanes = 128
    gather = jnp.where(iota((width, lanes), 0) // size == iota((width, lanes), 1), 1.0, 0.0)
    gather = gather.astype(BF16)
    spread = jnp.where(iota((lanes, width), 1) // size == iota((lanes, width), 0), 1.0, 0.0)
    spread = spread.astype(BF16)

    def step(z, carry):
        at = pl.multiple_of(z * spots, spots)
        query = queries[pl.ds(at, spots), :]
        product = keys[...].reshape(depth, spots, width) * query[None]
        product = product.reshape(tokens, width)
        high = product.astype(BF16)
        low = (product - high.astype(F32)).astype(BF16)
        scores = (dot(high, gather) + dot(low, gather)) * size ** (-0.5)
        scores = scores.reshape(depth, spots, lanes)
        exponent = jnp.exp(scores - jnp.max(scores, axis=0, keepdims=True))
        probs = exponent / jnp.sum(exponent, axis=0, keepdims=True)
        wide = dot(probs.reshape(tokens, lanes).astype(BF16), spread)
        context[pl.ds(at, spots), :] = jnp.sum(
            (wide * values[...]).reshape(depth, spots, width), axis=0
        )
        return carry

    lax.fori_loop(0, depth, step, 0)
    out[...] = (x + dot(context[...].astype(BF16), wo[...])).astype(BF16)


def decode(depth, block, gain, wqk, wv, wo):
    whole = pl.BlockSpec(memory_space=pltpu.VMEM)
    return pl.pallas_call(
        functools.partial(decode_kernel, depth),
        in_specs=[whole] * 5,
        out_specs=whole,
        out_shape=jax.ShapeDtypeStruct(block.shape, BF16),
        scratch_shapes=[pltpu.VMEM(block.shape, F32)] * 4,
        compiler_params=pltpu.CompilerParams(vmem_limit_bytes=40 << 20),
        name="decode",
    )(block, gain, wqk, wv, wo)


def per_device(
    volume,
    vis_mask,
    enc_gain,
    enc_wqk,
    enc_wv,
    enc_wo,
    final_gain,
    embed_w,
    mask_token,
    depth_pos,
    row_pos,
    col_pos,
    dec_gain,
    dec_wqk,
    dec_wv,
    dec_wo,
):
    _, plane_rows, plane_cols, width = volume.shape
    tokens = plane_rows * plane_cols
    mask = vis_mask.reshape(1, tokens)
    sent, rows = project(
        mask, volume.reshape(tokens, width), enc_gain.reshape(1, width), enc_wqk, enc_wv
    )
    mine = lax.all_to_all(sent, ("slab", "y"), split_axis=0, concat_axis=0, tiled=True)
    other = lax.ppermute(mine[:, :KV_ROWS, :], "half", [(0, 1), (1, 0)])
    counts = jnp.concatenate([mine[:, MOST, 0], other[:, MOST, 0]]).astype(jnp.int32)
    window_tokens = WIN_SLABS * tokens * lax.axis_size("y") * lax.axis_size("half")
    context = attend(counts, mine, other, window_tokens // 4)
    context = lax.all_to_all(context, ("slab", "y"), split_axis=0, concat_axis=0, tiled=True)
    streams = merge(
        plane_rows,
        mask,
        rows,
        context,
        enc_wo,
        final_gain.reshape(1, width),
        embed_w,
        mask_token.reshape(1, -1),
        depth_pos,
        row_pos,
        col_pos,
    )
    slabs = ("win", "slab")
    depth = depth_pos.shape[0]
    columns = lax.all_to_all(streams, slabs, split_axis=0, concat_axis=0, tiled=True)
    columns = decode(depth, columns, dec_gain.reshape(1, -1), dec_wqk, dec_wv, dec_wo)
    decoded = lax.all_to_all(columns, slabs, split_axis=0, concat_axis=0, tiled=True)
    return decoded.reshape(1, plane_rows, plane_cols, -1)


def solution(mesh):
    slabs, groups = mesh.devices.shape
    split = Mesh(
        mesh.devices.reshape(slabs // WIN_SLABS, WIN_SLABS, groups // 2, 2),
        ("win", "slab", "y", "half"),
    )
    placed = (
        P(("win", "slab"), ("y", "half"), None, None),
        P(("win", "slab"), ("y", "half"), None),
    ) + (P(),) * 14
    return jax.shard_map(
        per_device,
        mesh=split,
        in_specs=placed,
        out_specs=P(("win", "slab"), ("y", "half"), None, None),
        check_vma=False,
    )
```

```python
import functools

import jax
import jax.numpy as jnp
from jax import lax
from jax.experimental import pallas as pl
from jax.experimental.pallas import tpu as pltpu
from jax.sharding import Mesh, PartitionSpec as P

HEADS = 16
DHEADS = 16
WIN_SLABS = 8
MOST = 192
HALF = MOST // 2
COUNT_ROWS = 16
KV_ROWS = MOST + COUNT_ROWS
SEND_ROWS = KV_ROWS + HALF
QUAD = 4
LOG2E = 1.4426950408889634
F32 = jnp.float32
BF16 = jnp.bfloat16
MESH = pl.DeviceIdType.MESH


def dot(a, b):
    return lax.dot_general(a, b, (((1,), (0,)), ((), ())), preferred_element_type=F32)


def dot_nt(a, b):
    return lax.dot_general(a, b, (((1,), (1,)), ((), ())), preferred_element_type=F32)


def norm(values, gain):
    average = jnp.mean(values, axis=-1, keepdims=True)
    centered = values - average
    variance = jnp.mean(centered * centered, axis=-1, keepdims=True)
    return centered * lax.rsqrt(variance + 1e-05) * gain.astype(F32)


def iota(shape, dim):
    return lax.broadcasted_iota(jnp.int32, shape, dim)


def project_kernel(mask, volume, gain, wq, wk, wv, sent, rows, normed):
    tokens = volume.shape[0]

    @pl.when(pl.program_id(0) == 0)
    def _():
        seen = mask[...] == 1
        seen_rows = jnp.broadcast_to(jnp.where(seen, 1.0, 0.0), (16, tokens)).astype(BF16)
        upper = jnp.where(iota((tokens, tokens), 0) <= iota((tokens, tokens), 1), 1.0, 0.0)
        rank = dot(seen_rows, upper.astype(BF16))[0:1, :].astype(jnp.int32) - 1
        rank = jnp.where(seen, rank, -1)
        pick = jnp.where(iota((MOST, tokens), 0) == rank, 1.0, 0.0).astype(BF16)
        row_data = dot(pick, volume[...])
        rows[...] = row_data.astype(BF16)
        normed[...] = norm(row_data, gain[...]).astype(BF16)

    count = jnp.sum(jnp.where(mask[...] == 1, 1.0, 0.0), axis=1, keepdims=True)
    x = normed[...]
    size = wq.shape[1] // QUAD
    q = dot(x, wq[...]) * (size ** (-0.5) * LOG2E)
    k = dot(x, wk[...])
    v = dot(x, wv[...])
    for i in range(QUAD):
        part = slice(i * size, (i + 1) * size)
        sent[i, 0:MOST, :] = jnp.concatenate([k[:, part], v[:, part]], axis=1).astype(BF16)
        sent[i, MOST:KV_ROWS, :] = jnp.broadcast_to(count, (COUNT_ROWS, 2 * size)).astype(BF16)
        sent[i, KV_ROWS:SEND_ROWS, :] = jnp.concatenate(
            [q[0:HALF, part], q[HALF:MOST, part]], axis=1
        ).astype(BF16)


def project(mask, volume, gain, wqk, wv):
    tokens, width = volume.shape
    steps = HEADS // QUAD
    cols = width // steps
    lanes = 2 * (width // HEADS)
    return pl.pallas_call(
        project_kernel,
        grid=(steps,),
        in_specs=[
            pl.BlockSpec((1, tokens), lambda j: (0, 0)),
            pl.BlockSpec((tokens, width), lambda j: (0, 0)),
            pl.BlockSpec((1, width), lambda j: (0, 0)),
            pl.BlockSpec((width, cols), lambda j: (0, j)),
            pl.BlockSpec((width, cols), lambda j: (0, j + steps)),
            pl.BlockSpec((width, cols), lambda j: (0, j)),
        ],
        out_specs=[
            pl.BlockSpec((QUAD, SEND_ROWS, lanes), lambda j: (j, 0, 0)),
            pl.BlockSpec((MOST, width), lambda j: (0, 0)),
        ],
        out_shape=[
            jax.ShapeDtypeStruct((HEADS, SEND_ROWS, lanes), BF16),
            jax.ShapeDtypeStruct((MOST, width), BF16),
        ],
        scratch_shapes=[pltpu.VMEM((MOST, width), BF16)],
        compiler_params=pltpu.CompilerParams(vmem_limit_bytes=40 << 20),
        name="project",
    )(mask, volume, gain, wqk, wqk, wv)


TILE = 256


def attend_kernel(counts, mine, other, out, packed, queries, keys, values, results):
    blocks = mine.shape[0]
    lanes = mine.shape[2]
    size = lanes // 2
    total = keys.shape[0]
    half = total // 2
    zero = jnp.zeros((MOST, size), F32)
    offset = 0
    starts = []
    for i in range(2 * blocks):
        source = mine if i < blocks else other
        packed[pl.ds(offset, MOST), :] = source[i % blocks, 0:MOST, :].astype(F32)
        if i < blocks:
            starts.append(offset)
        offset = offset + counts[i]
    for i in range(0, total, TILE):
        both = packed[i : i + TILE, :]
        keys[i : i + TILE, :] = both.astype(BF16)
        values[i : i + TILE, :] = jnp.where(iota((TILE, lanes), 1) < size, 1.0, both).astype(BF16)
    for i in range(blocks):
        q = mine[i, KV_ROWS:SEND_ROWS, :].astype(F32)
        q = jnp.concatenate([q[:, :size], q[:, size:]], axis=0)
        packed[pl.ds(starts[i], MOST), :] = jnp.concatenate([q, zero], axis=1)
    for i in range(0, half, TILE):
        queries[i : i + TILE, :] = packed[i : i + TILE, :].astype(BF16)
    results[half:, :] = jnp.zeros((results.shape[0] - half, lanes), F32)

    def step(t, carry):
        at = pl.multiple_of(t * TILE, TILE)
        scores = dot_nt(queries[pl.ds(at, TILE), :], keys[...])
        top = jnp.max(scores, axis=-1, keepdims=True)
        weight = jnp.exp2(scores - top).astype(BF16)
        mixed = dot(weight, values[...])
        results[pl.ds(at, TILE), :] = mixed / pltpu.roll(mixed, size, 1)
        return carry

    lax.fori_loop(0, half // TILE, step, 0)
    for i in range(blocks):
        block = results[pl.ds(starts[i], MOST), :][:, size:]
        out[i, :, :] = jnp.concatenate([block[0:HALF], block[HALF:MOST]], axis=1).astype(BF16)


def attend(counts, mine, other, total):
    blocks, _, lanes = mine.shape
    whole = pl.BlockSpec(memory_space=pltpu.VMEM)
    return pl.pallas_call(
        attend_kernel,
        in_specs=[pl.BlockSpec(memory_space=pltpu.SMEM), whole, whole],
        out_specs=whole,
        out_shape=jax.ShapeDtypeStruct((blocks, HALF, lanes), BF16),
        scratch_shapes=[
            pltpu.VMEM((total + MOST, lanes), F32),
            pltpu.VMEM((total // 2, lanes), BF16),
            pltpu.VMEM((total, lanes), BF16),
            pltpu.VMEM((total, lanes), BF16),
            pltpu.VMEM((total // 2 + MOST, lanes), F32),
        ],
        compiler_params=pltpu.CompilerParams(vmem_limit_bytes=48 << 20),
        name="attend",
    )(counts, mine, other)


def finish_kernel(
    plane_rows,
    context,
    mask,
    rows,
    gain,
    mask_token,
    depth_pos,
    row_pos,
    col_pos,
    dec_gain,
    wo_hbm,
    embed_hbm,
    wqk_hbm,
    wv_hbm,
    dec_wo_hbm,
    out,
    wo,
    embed,
    wqk,
    wv,
    dec_wo,
    landed,
    streams,
    columns,
    queries,
    keys,
    values,
    decoded,
    load_sem,
    head_send,
    head_recv,
    part_send,
    part_recv,
    back_send,
    back_recv,
):
    slab, y = lax.axis_index("slab"), lax.axis_index("y")
    y_count, slab_count = lax.axis_size("y"), lax.axis_size("slab")
    heads, _, lanes = context.shape
    depth, spots, dec_width = out.shape
    tokens = depth * spots
    plane_cols = tokens // plane_rows
    head = slab * y_count + y
    level = lax.axis_index("win") * slab_count + slab
    size = lanes // 2

    loads = []
    for i, (source, target) in enumerate(
        ((wo_hbm, wo), (embed_hbm, embed), (wqk_hbm, wqk), (wv_hbm, wv), (dec_wo_hbm, dec_wo))
    ):
        load = pltpu.make_async_copy(source, target, load_sem.at[i])
        load.start()
        loads.append(load)

    def head_device(i):
        peer = lax.rem(head + i, heads)
        return peer, {"slab": peer // y_count, "y": lax.rem(peer, y_count)}

    def level_device(i):
        peer = lax.rem(level + i, depth)
        return peer, {"win": peer // slab_count, "slab": lax.rem(peer, slab_count)}

    barrier = pltpu.get_barrier_semaphore()
    for i in range(1, heads):
        _, place = head_device(i)
        pl.semaphore_signal(barrier, inc=1, device_id=place, device_id_type=MESH)
    for i in range(1, depth):
        _, place = level_device(i)
        pl.semaphore_signal(barrier, inc=1, device_id=place, device_id_type=MESH)
    pl.semaphore_wait(barrier, heads + depth - 2)

    head_copies = []
    for i in range(1, heads):
        peer, place = head_device(i)
        copy = pltpu.make_async_remote_copy(
            src_ref=context.at[peer],
            dst_ref=landed.at[head],
            send_sem=head_send.at[i],
            recv_sem=head_recv.at[i],
            device_id=place,
            device_id_type=MESH,
        )
        copy.start()
        head_copies.append(copy)
    landed[head] = context[head]

    seen = jnp.broadcast_to(jnp.where(mask[...] == 1, 1.0, 0.0), (16, tokens)).astype(BF16)
    down, across = iota((tokens, tokens), 0), iota((tokens, tokens), 1)
    rank = dot_nt(jnp.where(across <= down, 1.0, 0.0).astype(BF16), seen)[:, 0:1]
    shown = dot_nt(jnp.where(across == down, 1.0, 0.0).astype(BF16), seen)[:, 0:1] > 0.5
    rank = jnp.where(shown, rank.astype(jnp.int32) - 1, -1)
    place = jnp.where(iota((tokens, MOST), 1) == rank, 1.0, 0.0).astype(BF16)
    grp = y * lax.axis_size("half") + lax.axis_index("half")
    depths = depth_pos[...].astype(F32)
    chosen = jnp.where(iota(depths.shape, 0) == level, depths, 0.0)
    chosen = jnp.sum(chosen, axis=0, keepdims=True)
    row_count, col_count = row_pos.shape[0], col_pos.shape[0]
    row = iota((tokens, row_count), 0) // plane_cols + grp * plane_rows
    row_hot = jnp.where(iota((tokens, row_count), 1) == row, 1.0, 0.0).astype(BF16)
    row_part = dot(row_hot, row_pos[...])
    col = iota((tokens, col_count), 0) % plane_cols
    col_hot = jnp.where(iota((tokens, col_count), 1) == col, 1.0, 0.0).astype(BF16)
    col_part = dot(col_hot, col_pos[...])

    loads[0].wait()
    loads[1].wait()
    for copy in head_copies:
        copy.wait()
    tiles = []
    for j in range(0, heads, 2):
        a, b = landed[j], landed[j + 1]
        tiles.append(
            jnp.concatenate(
                [
                    jnp.concatenate([a[:, :size], b[:, :size]], axis=1),
                    jnp.concatenate([a[:, size:], b[:, size:]], axis=1),
                ],
                axis=0,
            )
        )
    mixed = rows[...].astype(F32) + dot(jnp.concatenate(tiles, axis=1), wo[...])
    encoded = norm(mixed, gain[...]).astype(BF16)
    embedded = dot(encoded, embed[...]).astype(BF16)
    stream = dot(place, embedded)
    stream = jnp.where(shown, stream, mask_token[...].astype(F32))
    stream = ((stream + chosen) + row_part) + col_part
    streams[...] = stream.reshape(depth, spots, dec_width).astype(BF16)

    def part_copy(i):
        peer, where = level_device(i)
        return pltpu.make_async_remote_copy(
            src_ref=streams.at[peer],
            dst_ref=columns.at[level],
            send_sem=part_send.at[i],
            recv_sem=part_recv.at[i],
            device_id=where,
            device_id_type=MESH,
        )

    def back_copy(i):
        peer, where = level_device(i)
        return pltpu.make_async_remote_copy(
            src_ref=decoded.at[peer],
            dst_ref=out.at[level],
            send_sem=back_send.at[i],
            recv_sem=back_recv.at[i],
            device_id=where,
            device_id_type=MESH,
        )

    def start_part(i, carry):
        part_copy(i).start()
        return carry

    lax.fori_loop(1, depth, start_part, 0)
    columns[level] = streams[level]
    for load in loads[2:]:
        load.wait()

    def wait_part(i, carry):
        part_copy(i).wait()
        return carry

    lax.fori_loop(1, depth, wait_part, 0)
    x = columns[...].astype(F32).reshape(tokens, dec_width)
    normed = norm(x, dec_gain[...]).astype(BF16)
    shape = (depth, spots, dec_width)
    queries[...] = dot(normed, wqk[:, :dec_width]).astype(BF16).astype(F32).reshape(shape)
    keys[...] = dot(normed, wqk[:, dec_width:]).astype(BF16).astype(F32).reshape(shape)
    values[...] = dot(normed, wv[...]).astype(BF16).astype(F32).reshape(shape)
    dec_size = dec_width // DHEADS
    wide = 128
    gather = jnp.where(
        iota((dec_width, wide), 0) // dec_size == iota((dec_width, wide), 1), 1.0, 0.0
    ).astype(BF16)
    spread = jnp.where(
        iota((wide, dec_width), 1) // dec_size == iota((wide, dec_width), 0), 1.0, 0.0
    ).astype(BF16)

    def decode(z):
        product = (keys[...] * queries[z][None]).reshape(tokens, dec_width)
        high = product.astype(BF16)
        low = (product - high.astype(F32)).astype(BF16)
        scores = (dot(high, gather) + dot(low, gather)) * dec_size ** (-0.5)
        scores = scores.reshape(depth, spots, wide)
        exponent = jnp.exp(scores - jnp.max(scores, axis=0, keepdims=True))
        probs = exponent / jnp.sum(exponent, axis=0, keepdims=True)
        probs = dot(probs.reshape(tokens, wide).astype(BF16), spread).reshape(shape)
        result = jnp.sum(probs * values[...], axis=0).astype(BF16)
        return (columns[z].astype(F32) + dot(result, dec_wo[...])).astype(BF16)

    def step(i, carry):
        z = lax.rem(level + i, depth)
        decoded[z] = decode(z)
        back_copy(i).start()
        return carry

    lax.fori_loop(1, depth, step, 0)
    out[level] = decode(level)

    def wait_back(i, carry):
        back_copy(i).wait()
        return carry

    lax.fori_loop(1, depth, wait_back, 0)


def finish(plane_rows, depth, context, mask, rows, *others):
    tokens = mask.shape[1]
    weights = others[-5:]
    dec_width = weights[1].shape[1]
    heads = context.shape[0]
    whole = pl.BlockSpec(memory_space=pltpu.VMEM)
    shape = (depth, tokens // depth, dec_width)
    dma = pltpu.SemaphoreType.DMA
    return pl.pallas_call(
        functools.partial(finish_kernel, plane_rows),
        in_specs=[whole] * 9 + [pl.BlockSpec(memory_space=pl.ANY)] * 5,
        out_specs=whole,
        out_shape=jax.ShapeDtypeStruct(shape, BF16),
        scratch_shapes=[pltpu.VMEM(w.shape, BF16) for w in weights]
        + [
            pltpu.VMEM(context.shape, BF16),
            pltpu.VMEM(shape, BF16),
            pltpu.VMEM(shape, BF16),
            pltpu.VMEM(shape, F32),
            pltpu.VMEM(shape, F32),
            pltpu.VMEM(shape, F32),
            pltpu.VMEM(shape, BF16),
            dma((5,)),
            dma((heads,)),
            dma((heads,)),
            dma((depth,)),
            dma((depth,)),
            dma((depth,)),
            dma((depth,)),
        ],
        compiler_params=pltpu.CompilerParams(
            vmem_limit_bytes=48 << 20, collective_id=1, has_side_effects=True
        ),
        name="finish",
    )(context, mask, rows, *others)


def per_device(
    volume,
    vis_mask,
    enc_gain,
    enc_wqk,
    enc_wv,
    enc_wo,
    final_gain,
    embed_w,
    mask_token,
    depth_pos,
    row_pos,
    col_pos,
    dec_gain,
    dec_wqk,
    dec_wv,
    dec_wo,
):
    _, plane_rows, plane_cols, width = volume.shape
    tokens = plane_rows * plane_cols
    mask = vis_mask.reshape(1, tokens)
    sent, rows = project(
        mask, volume.reshape(tokens, width), enc_gain.reshape(1, width), enc_wqk, enc_wv
    )
    mine = lax.all_to_all(sent, ("slab", "y"), split_axis=0, concat_axis=0, tiled=True)
    other = lax.ppermute(mine[:, :KV_ROWS, :], "half", [(0, 1), (1, 0)])
    counts = jnp.concatenate([mine[:, MOST, 0], other[:, MOST, 0]]).astype(jnp.int32)
    window_tokens = WIN_SLABS * tokens * lax.axis_size("y") * lax.axis_size("half")
    context = attend(counts, mine, other, window_tokens // 4)
    decoded = finish(
        plane_rows,
        depth_pos.shape[0],
        context,
        mask,
        rows,
        final_gain.reshape(1, width),
        mask_token.reshape(1, -1),
        depth_pos,
        row_pos,
        col_pos,
        dec_gain.reshape(1, -1),
        enc_wo,
        embed_w,
        dec_wqk,
        dec_wv,
        dec_wo,
    )
    return decoded.reshape(1, plane_rows, plane_cols, -1)


def solution(mesh):
    slabs, groups = mesh.devices.shape
    split = Mesh(
        mesh.devices.reshape(slabs // WIN_SLABS, WIN_SLABS, groups // 2, 2),
        ("win", "slab", "y", "half"),
    )
    placed = (
        P(("win", "slab"), ("y", "half"), None, None),
        P(("win", "slab"), ("y", "half"), None),
    ) + (P(),) * 14
    return jax.shard_map(
        per_device,
        mesh=split,
        in_specs=placed,
        out_specs=P(("win", "slab"), ("y", "half"), None, None),
        check_vma=False,
    )
```

```python
import functools

import jax
import jax.numpy as jnp
from jax import lax
from jax.experimental import pallas as pl
from jax.experimental.pallas import tpu as pltpu
from jax.sharding import Mesh, PartitionSpec as P

HEADS = 16
DHEADS = 16
WIN_SLABS = 8
MOST = 192
HALF = MOST // 2
COUNT_ROWS = 16
KV_ROWS = MOST + COUNT_ROWS
SEND_ROWS = KV_ROWS + HALF
QUAD = 4
LOG2E = 1.4426950408889634
F32 = jnp.float32
BF16 = jnp.bfloat16
MESH = pl.DeviceIdType.MESH


def dot(a, b):
    return lax.dot_general(a, b, (((1,), (0,)), ((), ())), preferred_element_type=F32)


def dot_nt(a, b):
    return lax.dot_general(a, b, (((1,), (1,)), ((), ())), preferred_element_type=F32)


def norm(values, gain):
    average = jnp.mean(values, axis=-1, keepdims=True)
    centered = values - average
    variance = jnp.mean(centered * centered, axis=-1, keepdims=True)
    return centered * lax.rsqrt(variance + 1e-05) * gain.astype(F32)


def iota(shape, dim):
    return lax.broadcasted_iota(jnp.int32, shape, dim)


def mask_row(mask):
    return jnp.concatenate([mask[0, r : r + 1, :] for r in range(mask.shape[1])], axis=1)


def project_kernel(
    mask,
    gain,
    volume_hbm,
    wqk_hbm,
    wv_hbm,
    rows,
    mine,
    other,
    volume,
    wq,
    wk,
    wv,
    sent,
    load_sem,
    send_sem,
    recv_sem,
    pass_send,
    pass_recv,
):
    slab, y, side = lax.axis_index("slab"), lax.axis_index("y"), lax.axis_index("half")
    y_count = lax.axis_size("y")
    tokens, width = volume.shape
    quads, _, cols = wq.shape
    head = slab * y_count + y
    own_quad = head // QUAD
    order = [(t + 1) % quads for t in range(quads)]

    first = pltpu.make_async_copy(volume_hbm, volume, load_sem.at[3 * quads])
    first.start()
    loads = []
    for t in range(quads):
        quad = lax.rem(own_quad + order[t], quads)
        at = pl.multiple_of(quad * cols, cols)
        group = [
            pltpu.make_async_copy(
                wqk_hbm.at[:, pl.ds(at, cols)], wq.at[t], load_sem.at[3 * t]
            ),
            pltpu.make_async_copy(
                wqk_hbm.at[:, pl.ds(at + width, cols)], wk.at[t], load_sem.at[3 * t + 1]
            ),
            pltpu.make_async_copy(
                wv_hbm.at[:, pl.ds(at, cols)], wv.at[t], load_sem.at[3 * t + 2]
            ),
        ]
        for load in group:
            load.start()
        loads.append(group)

    def place(peer):
        return {"slab": peer // y_count, "y": lax.rem(peer, y_count)}

    barrier = pltpu.get_barrier_semaphore()
    for i in range(1, HEADS):
        peer = lax.rem(head + i, HEADS)
        pl.semaphore_signal(barrier, inc=1, device_id=place(peer), device_id_type=MESH)
    pl.semaphore_signal(barrier, inc=1, device_id={"half": 1 - side}, device_id_type=MESH)

    seen = mask_row(mask) == 1
    count = jnp.sum(jnp.where(seen, 1.0, 0.0), axis=1, keepdims=True)
    seen_rows = jnp.broadcast_to(jnp.where(seen, 1.0, 0.0), (16, tokens)).astype(BF16)
    upper = jnp.where(iota((tokens, tokens), 0) <= iota((tokens, tokens), 1), 1.0, 0.0)
    rank = dot(seen_rows, upper.astype(BF16))[0:1, :].astype(jnp.int32) - 1
    rank = jnp.where(seen, rank, -1)
    pick = jnp.where(iota((MOST, tokens), 0) == rank, 1.0, 0.0).astype(BF16)
    first.wait()
    row_data = dot(pick, volume[...])
    rows[...] = row_data.astype(BF16)
    x = norm(row_data, gain[...].astype(F32).reshape(1, width)).astype(BF16)
    size = cols // QUAD
    counts = jnp.broadcast_to(count, (COUNT_ROWS, 2 * size)).astype(BF16)
    pl.semaphore_wait(barrier, HEADS)

    def send(peer):
        return pltpu.make_async_remote_copy(
            src_ref=sent.at[peer],
            dst_ref=mine.at[head],
            send_sem=send_sem.at[peer],
            recv_sem=recv_sem.at[head],
            device_id=place(peer),
            device_id_type=MESH,
        )

    def arrival(peer):
        return pltpu.make_async_remote_copy(
            src_ref=sent.at[peer],
            dst_ref=mine.at[peer],
            send_sem=send_sem.at[peer],
            recv_sem=recv_sem.at[peer],
            device_id=place(peer),
            device_id_type=MESH,
        )

    def hand_over(peer):
        return pltpu.make_async_remote_copy(
            src_ref=mine.at[peer, pl.ds(0, KV_ROWS)],
            dst_ref=other.at[peer],
            send_sem=pass_send.at[peer],
            recv_sem=pass_recv.at[peer],
            device_id={"half": 1 - side},
            device_id_type=MESH,
        )

    for t in range(quads):
        for load in loads[t]:
            load.wait()
        quad = lax.rem(own_quad + order[t], quads)
        q = dot(x, wq[t]) * (size ** (-0.5) * LOG2E)
        k = dot(x, wk[t])
        v = dot(x, wv[t])
        for i in range(QUAD):
            part = slice(i * size, (i + 1) * size)
            peer = quad * QUAD + i
            sent[peer, 0:MOST, :] = jnp.concatenate([k[:, part], v[:, part]], axis=1).astype(BF16)
            sent[peer, MOST:KV_ROWS, :] = counts
            sent[peer, KV_ROWS:SEND_ROWS, :] = jnp.concatenate(
                [q[0:HALF, part], q[HALF:MOST, part]], axis=1
            ).astype(BF16)
            if order[t] > 0:
                send(peer).start()
            else:

                @pl.when(peer != head)
                def _():
                    send(peer).start()

    mine[head] = sent[head]
    hand_over(head).start()
    for t in range(quads):
        quad = lax.rem(own_quad - order[t] + quads, quads)
        for i in range(QUAD):
            peer = quad * QUAD + i
            if order[t] > 0:
                arrival(peer).wait_recv()
                hand_over(peer).start()
            else:

                @pl.when(peer != head)
                def _():
                    arrival(peer).wait_recv()
                    hand_over(peer).start()

    for i in range(1, HEADS):
        send(lax.rem(head + i, HEADS)).wait_send()
    for i in range(HEADS):
        hand_over(i).wait()


def project(mask, gain, volume, wqk, wv):
    tokens, width = volume.shape
    quads = HEADS // QUAD
    cols = width // quads
    lanes = 2 * (width // HEADS)
    whole = pl.BlockSpec(memory_space=pltpu.VMEM)
    dma = pltpu.SemaphoreType.DMA
    return pl.pallas_call(
        project_kernel,
        in_specs=[whole] * 2 + [pl.BlockSpec(memory_space=pl.ANY)] * 3,
        out_specs=[whole] * 3,
        out_shape=[
            jax.ShapeDtypeStruct((MOST, width), BF16),
            jax.ShapeDtypeStruct((HEADS, SEND_ROWS, lanes), BF16),
            jax.ShapeDtypeStruct((HEADS, KV_ROWS, lanes), BF16),
        ],
        scratch_shapes=[
            pltpu.VMEM((tokens, width), BF16),
            pltpu.VMEM((quads, width, cols), BF16),
            pltpu.VMEM((quads, width, cols), BF16),
            pltpu.VMEM((quads, width, cols), BF16),
            pltpu.VMEM((HEADS, SEND_ROWS, lanes), BF16),
            dma((3 * quads + 1,)),
            dma((HEADS,)),
            dma((HEADS,)),
            dma((HEADS,)),
            dma((HEADS,)),
        ],
        compiler_params=pltpu.CompilerParams(
            vmem_limit_bytes=52 << 20, collective_id=0, has_side_effects=True
        ),
        name="project",
    )(mask, gain, volume, wqk, wv)


TILE = 256


def attend_kernel(counts, mine, other, out, packed, queries, keys, values, results):
    blocks = mine.shape[0]
    lanes = mine.shape[2]
    size = lanes // 2
    total = keys.shape[0]
    half = total // 2
    zero = jnp.zeros((MOST, size), F32)
    offset = 0
    starts = []
    for i in range(2 * blocks):
        source = mine if i < blocks else other
        packed[pl.ds(offset, MOST), :] = source[i % blocks, 0:MOST, :].astype(F32)
        if i < blocks:
            starts.append(offset)
        offset = offset + counts[i]
    for i in range(0, total, TILE):
        both = packed[i : i + TILE, :]
        keys[i : i + TILE, :] = both.astype(BF16)
        values[i : i + TILE, :] = jnp.where(iota((TILE, lanes), 1) < size, 1.0, both).astype(BF16)
    for i in range(blocks):
        q = mine[i, KV_ROWS:SEND_ROWS, :].astype(F32)
        q = jnp.concatenate([q[:, :size], q[:, size:]], axis=0)
        packed[pl.ds(starts[i], MOST), :] = jnp.concatenate([q, zero], axis=1)
    for i in range(0, half, TILE):
        queries[i : i + TILE, :] = packed[i : i + TILE, :].astype(BF16)
    results[half:, :] = jnp.zeros((results.shape[0] - half, lanes), F32)

    def step(t, carry):
        at = pl.multiple_of(t * TILE, TILE)
        scores = dot_nt(queries[pl.ds(at, TILE), :], keys[...])
        top = jnp.max(scores, axis=-1, keepdims=True)
        weight = jnp.exp2(scores - top).astype(BF16)
        mixed = dot(weight, values[...])
        results[pl.ds(at, TILE), :] = mixed / pltpu.roll(mixed, size, 1)
        return carry

    lax.fori_loop(0, half // TILE, step, 0)
    for i in range(blocks):
        block = results[pl.ds(starts[i], MOST), :][:, size:]
        out[i, :, :] = jnp.concatenate([block[0:HALF], block[HALF:MOST]], axis=1).astype(BF16)


def attend(counts, mine, other, total):
    blocks, _, lanes = mine.shape
    whole = pl.BlockSpec(memory_space=pltpu.VMEM)
    return pl.pallas_call(
        attend_kernel,
        in_specs=[pl.BlockSpec(memory_space=pltpu.SMEM), whole, whole],
        out_specs=whole,
        out_shape=jax.ShapeDtypeStruct((blocks, HALF, lanes), BF16),
        scratch_shapes=[
            pltpu.VMEM((total + MOST, lanes), F32),
            pltpu.VMEM((total // 2, lanes), BF16),
            pltpu.VMEM((total, lanes), BF16),
            pltpu.VMEM((total, lanes), BF16),
            pltpu.VMEM((total // 2 + MOST, lanes), F32),
        ],
        compiler_params=pltpu.CompilerParams(vmem_limit_bytes=48 << 20),
        name="attend",
    )(counts, mine, other)


def finish_kernel(
    plane_rows,
    context,
    mask,
    rows,
    gain,
    mask_token,
    depth_pos,
    row_pos,
    col_pos,
    dec_gain,
    wo_hbm,
    embed_hbm,
    wqk_hbm,
    wv_hbm,
    dec_wo_hbm,
    out,
    wo,
    embed,
    wqk,
    wv,
    dec_wo,
    landed,
    streams,
    columns,
    queries,
    keys,
    values,
    decoded,
    load_sem,
    head_send,
    head_recv,
    part_send,
    part_recv,
    back_send,
    back_recv,
):
    slab, y = lax.axis_index("slab"), lax.axis_index("y")
    y_count, slab_count = lax.axis_size("y"), lax.axis_size("slab")
    heads, _, lanes = context.shape
    depth, spots, dec_width = out.shape
    tokens = depth * spots
    plane_cols = tokens // plane_rows
    head = slab * y_count + y
    level = lax.axis_index("win") * slab_count + slab
    size = lanes // 2

    loads = []
    for i, (source, target) in enumerate(
        ((wo_hbm, wo), (embed_hbm, embed), (wqk_hbm, wqk), (wv_hbm, wv), (dec_wo_hbm, dec_wo))
    ):
        load = pltpu.make_async_copy(source, target, load_sem.at[i])
        load.start()
        loads.append(load)

    def head_device(i):
        peer = lax.rem(head + i, heads)
        return peer, {"slab": peer // y_count, "y": lax.rem(peer, y_count)}

    def level_device(i):
        peer = lax.rem(level + i, depth)
        return peer, {"win": peer // slab_count, "slab": lax.rem(peer, slab_count)}

    barrier = pltpu.get_barrier_semaphore()
    for i in range(1, heads):
        _, place = head_device(i)
        pl.semaphore_signal(barrier, inc=1, device_id=place, device_id_type=MESH)
    for i in range(1, depth):
        _, place = level_device(i)
        pl.semaphore_signal(barrier, inc=1, device_id=place, device_id_type=MESH)
    pl.semaphore_wait(barrier, heads + depth - 2)

    head_copies = []
    for i in range(1, heads):
        peer, place = head_device(i)
        copy = pltpu.make_async_remote_copy(
            src_ref=context.at[peer],
            dst_ref=landed.at[head],
            send_sem=head_send.at[i],
            recv_sem=head_recv.at[i],
            device_id=place,
            device_id_type=MESH,
        )
        copy.start()
        head_copies.append(copy)
    landed[head] = context[head]

    seen = jnp.where(mask_row(mask) == 1, 1.0, 0.0)
    seen = jnp.broadcast_to(seen, (16, tokens)).astype(BF16)
    down, across = iota((tokens, tokens), 0), iota((tokens, tokens), 1)
    rank = dot_nt(jnp.where(across <= down, 1.0, 0.0).astype(BF16), seen)[:, 0:1]
    shown = dot_nt(jnp.where(across == down, 1.0, 0.0).astype(BF16), seen)[:, 0:1] > 0.5
    rank = jnp.where(shown, rank.astype(jnp.int32) - 1, -1)
    place = jnp.where(iota((tokens, MOST), 1) == rank, 1.0, 0.0).astype(BF16)
    grp = y * lax.axis_size("half") + lax.axis_index("half")
    depths = depth_pos[...].astype(F32)
    chosen = jnp.where(iota(depths.shape, 0) == level, depths, 0.0)
    chosen = jnp.sum(chosen, axis=0, keepdims=True)
    row_count, col_count = row_pos.shape[0], col_pos.shape[0]
    row = iota((tokens, row_count), 0) // plane_cols + grp * plane_rows
    row_hot = jnp.where(iota((tokens, row_count), 1) == row, 1.0, 0.0).astype(BF16)
    row_part = dot(row_hot, row_pos[...])
    col = iota((tokens, col_count), 0) % plane_cols
    col_hot = jnp.where(iota((tokens, col_count), 1) == col, 1.0, 0.0).astype(BF16)
    col_part = dot(col_hot, col_pos[...])

    loads[0].wait()
    loads[1].wait()
    for copy in head_copies:
        copy.wait()
    tiles = []
    for j in range(0, heads, 2):
        a, b = landed[j], landed[j + 1]
        tiles.append(
            jnp.concatenate(
                [
                    jnp.concatenate([a[:, :size], b[:, :size]], axis=1),
                    jnp.concatenate([a[:, size:], b[:, size:]], axis=1),
                ],
                axis=0,
            )
        )
    mixed = rows[...].astype(F32) + dot(jnp.concatenate(tiles, axis=1), wo[...])
    encoded = norm(mixed, gain[...]).astype(BF16)
    embedded = dot(encoded, embed[...]).astype(BF16)
    stream = dot(place, embedded)
    stream = jnp.where(shown, stream, mask_token[...].astype(F32))
    stream = ((stream + chosen) + row_part) + col_part
    streams[...] = stream.reshape(depth, spots, dec_width).astype(BF16)

    def part_copy(i):
        peer, where = level_device(i)
        return pltpu.make_async_remote_copy(
            src_ref=streams.at[peer],
            dst_ref=columns.at[level],
            send_sem=part_send.at[i],
            recv_sem=part_recv.at[i],
            device_id=where,
            device_id_type=MESH,
        )

    def back_copy(i):
        peer, where = level_device(i)
        return pltpu.make_async_remote_copy(
            src_ref=decoded.at[peer],
            dst_ref=out.at[level],
            send_sem=back_send.at[i],
            recv_sem=back_recv.at[i],
            device_id=where,
            device_id_type=MESH,
        )

    def start_part(i, carry):
        part_copy(i).start()
        return carry

    lax.fori_loop(1, depth, start_part, 0)
    columns[level] = streams[level]
    for load in loads[2:]:
        load.wait()

    def wait_part(i, carry):
        part_copy(i).wait()
        return carry

    lax.fori_loop(1, depth, wait_part, 0)
    x = columns[...].astype(F32).reshape(tokens, dec_width)
    normed = norm(x, dec_gain[...]).astype(BF16)
    shape = (depth, spots, dec_width)
    queries[...] = dot(normed, wqk[:, :dec_width]).astype(BF16).astype(F32).reshape(shape)
    keys[...] = dot(normed, wqk[:, dec_width:]).astype(BF16).astype(F32).reshape(shape)
    values[...] = dot(normed, wv[...]).astype(BF16).astype(F32).reshape(shape)
    dec_size = dec_width // DHEADS
    wide = 128
    gather = jnp.where(
        iota((dec_width, wide), 0) // dec_size == iota((dec_width, wide), 1), 1.0, 0.0
    ).astype(BF16)
    spread = jnp.where(
        iota((wide, dec_width), 1) // dec_size == iota((wide, dec_width), 0), 1.0, 0.0
    ).astype(BF16)

    def decode(z):
        product = (keys[...] * queries[z][None]).reshape(tokens, dec_width)
        high = product.astype(BF16)
        low = (product - high.astype(F32)).astype(BF16)
        scores = (dot(high, gather) + dot(low, gather)) * dec_size ** (-0.5)
        scores = scores.reshape(depth, spots, wide)
        exponent = jnp.exp(scores - jnp.max(scores, axis=0, keepdims=True))
        probs = exponent / jnp.sum(exponent, axis=0, keepdims=True)
        probs = dot(probs.reshape(tokens, wide).astype(BF16), spread).reshape(shape)
        result = jnp.sum(probs * values[...], axis=0).astype(BF16)
        return (columns[z].astype(F32) + dot(result, dec_wo[...])).astype(BF16)

    def step(i, carry):
        z = lax.rem(level + i, depth)
        decoded[z] = decode(z)
        back_copy(i).start()
        return carry

    lax.fori_loop(1, depth, step, 0)
    out[level] = decode(level)

    def wait_back(i, carry):
        back_copy(i).wait()
        return carry

    lax.fori_loop(1, depth, wait_back, 0)


def finish(plane_rows, depth, context, mask, rows, *others):
    tokens = mask.shape[1] * mask.shape[2]
    weights = others[-5:]
    dec_width = weights[1].shape[1]
    heads = context.shape[0]
    whole = pl.BlockSpec(memory_space=pltpu.VMEM)
    shape = (depth, tokens // depth, dec_width)
    dma = pltpu.SemaphoreType.DMA
    return pl.pallas_call(
        functools.partial(finish_kernel, plane_rows),
        in_specs=[whole] * 9 + [pl.BlockSpec(memory_space=pl.ANY)] * 5,
        out_specs=whole,
        out_shape=jax.ShapeDtypeStruct(shape, BF16),
        scratch_shapes=[pltpu.VMEM(w.shape, BF16) for w in weights]
        + [
            pltpu.VMEM(context.shape, BF16),
            pltpu.VMEM(shape, BF16),
            pltpu.VMEM(shape, BF16),
            pltpu.VMEM(shape, F32),
            pltpu.VMEM(shape, F32),
            pltpu.VMEM(shape, F32),
            pltpu.VMEM(shape, BF16),
            dma((5,)),
            dma((heads,)),
            dma((heads,)),
            dma((depth,)),
            dma((depth,)),
            dma((depth,)),
            dma((depth,)),
        ],
        compiler_params=pltpu.CompilerParams(
            vmem_limit_bytes=48 << 20, collective_id=1, has_side_effects=True
        ),
        name="finish",
    )(context, mask, rows, *others)


def per_device(
    volume,
    vis_mask,
    enc_gain,
    enc_wqk,
    enc_wv,
    enc_wo,
    final_gain,
    embed_w,
    mask_token,
    depth_pos,
    row_pos,
    col_pos,
    dec_gain,
    dec_wqk,
    dec_wv,
    dec_wo,
):
    _, plane_rows, plane_cols, width = volume.shape
    tokens = plane_rows * plane_cols
    rows, mine, other = project(
        vis_mask, enc_gain, volume.reshape(tokens, width), enc_wqk, enc_wv
    )
    counts = jnp.concatenate([mine[:, MOST, 0], other[:, MOST, 0]]).astype(jnp.int32)
    window_tokens = WIN_SLABS * tokens * lax.axis_size("y") * lax.axis_size("half")
    context = attend(counts, mine, other, window_tokens // 4)
    decoded = finish(
        plane_rows,
        depth_pos.shape[0],
        context,
        vis_mask,
        rows,
        final_gain.reshape(1, width),
        mask_token.reshape(1, -1),
        depth_pos,
        row_pos,
        col_pos,
        dec_gain.reshape(1, -1),
        enc_wo,
        embed_w,
        dec_wqk,
        dec_wv,
        dec_wo,
    )
    return decoded.reshape(1, plane_rows, plane_cols, -1)


def solution(mesh):
    slabs, groups = mesh.devices.shape
    split = Mesh(
        mesh.devices.reshape(slabs // WIN_SLABS, WIN_SLABS, groups // 2, 2),
        ("win", "slab", "y", "half"),
    )
    placed = (
        P(("win", "slab"), ("y", "half"), None, None),
        P(("win", "slab"), ("y", "half"), None),
    ) + (P(),) * 14
    return jax.shard_map(
        per_device,
        mesh=split,
        in_specs=placed,
        out_specs=P(("win", "slab"), ("y", "half"), None, None),
        check_vma=False,
    )
```

```python
import functools

import jax
import jax.numpy as jnp
from jax import lax
from jax.experimental import pallas as pl
from jax.experimental.pallas import tpu as pltpu
from jax.sharding import Mesh, PartitionSpec as P

HEADS = 16
DHEADS = 16
WIN_SLABS = 8
MOST = 192
HALF = MOST // 2
COUNT_ROWS = 16
KV_ROWS = MOST + COUNT_ROWS
SEND_ROWS = KV_ROWS + HALF
QUAD = 4
LOG2E = 1.4426950408889634
F32 = jnp.float32
BF16 = jnp.bfloat16
MESH = pl.DeviceIdType.MESH


def dot(a, b):
    return lax.dot_general(a, b, (((1,), (0,)), ((), ())), preferred_element_type=F32)


def dot_nt(a, b):
    return lax.dot_general(a, b, (((1,), (1,)), ((), ())), preferred_element_type=F32)


def norm(values, gain):
    average = jnp.mean(values, axis=-1, keepdims=True)
    centered = values - average
    variance = jnp.mean(centered * centered, axis=-1, keepdims=True)
    return centered * lax.rsqrt(variance + 1e-05) * gain.astype(F32)


def iota(shape, dim):
    return lax.broadcasted_iota(jnp.int32, shape, dim)


def flip(position, bits, count):
    result, weight = 0, 1
    while weight < count:
        result = result + lax.rem(position // weight + bits // weight, 2) * weight
        weight *= 2
    return result


def mask_row(mask):
    return jnp.concatenate([mask[0, r : r + 1, :] for r in range(mask.shape[1])], axis=1)


def project_kernel(
    mask,
    gain,
    volume_hbm,
    wqk_hbm,
    wv_hbm,
    rows,
    mine,
    other,
    volume,
    wq,
    wk,
    wv,
    sent,
    load_sem,
    send_sem,
    recv_sem,
    pass_send,
    pass_recv,
):
    slab, y, side = lax.axis_index("slab"), lax.axis_index("y"), lax.axis_index("half")
    y_count = lax.axis_size("y")
    tokens, width = volume.shape
    quads, _, cols = wq.shape
    head = slab * y_count + y
    own_quad = head // QUAD
    order = [quads // 2 + t for t in range(quads // 2)] + list(range(quads // 2 - 1, -1, -1))

    first = pltpu.make_async_copy(volume_hbm, volume, load_sem.at[3 * quads])
    first.start()
    loads = []
    for t in range(quads):
        quad = flip(own_quad, order[t], quads)
        at = pl.multiple_of(quad * cols, cols)
        group = [
            pltpu.make_async_copy(
                wqk_hbm.at[:, pl.ds(at, cols)], wq.at[t], load_sem.at[3 * t]
            ),
            pltpu.make_async_copy(
                wqk_hbm.at[:, pl.ds(at + width, cols)], wk.at[t], load_sem.at[3 * t + 1]
            ),
            pltpu.make_async_copy(
                wv_hbm.at[:, pl.ds(at, cols)], wv.at[t], load_sem.at[3 * t + 2]
            ),
        ]
        for load in group:
            load.start()
        loads.append(group)

    def place(peer):
        return {"slab": peer // y_count, "y": lax.rem(peer, y_count)}

    barrier = pltpu.get_barrier_semaphore()
    for i in range(1, HEADS):
        peer = lax.rem(head + i, HEADS)
        pl.semaphore_signal(barrier, inc=1, device_id=place(peer), device_id_type=MESH)
    pl.semaphore_signal(barrier, inc=1, device_id={"half": 1 - side}, device_id_type=MESH)

    seen = mask_row(mask) == 1
    count = jnp.sum(jnp.where(seen, 1.0, 0.0), axis=1, keepdims=True)
    seen_rows = jnp.broadcast_to(jnp.where(seen, 1.0, 0.0), (16, tokens)).astype(BF16)
    upper = jnp.where(iota((tokens, tokens), 0) <= iota((tokens, tokens), 1), 1.0, 0.0)
    rank = dot(seen_rows, upper.astype(BF16))[0:1, :].astype(jnp.int32) - 1
    rank = jnp.where(seen, rank, -1)
    pick = jnp.where(iota((MOST, tokens), 0) == rank, 1.0, 0.0).astype(BF16)
    first.wait()
    row_data = dot(pick, volume[...])
    rows[...] = row_data.astype(BF16)
    x = norm(row_data, gain[...].astype(F32).reshape(1, width)).astype(BF16)
    size = cols // QUAD
    counts = jnp.broadcast_to(count, (COUNT_ROWS, 2 * size)).astype(BF16)
    pl.semaphore_wait(barrier, HEADS)

    def send(peer):
        return pltpu.make_async_remote_copy(
            src_ref=sent.at[peer],
            dst_ref=mine.at[head],
            send_sem=send_sem.at[peer],
            recv_sem=recv_sem.at[head],
            device_id=place(peer),
            device_id_type=MESH,
        )

    def arrival(peer):
        return pltpu.make_async_remote_copy(
            src_ref=sent.at[peer],
            dst_ref=mine.at[peer],
            send_sem=send_sem.at[peer],
            recv_sem=recv_sem.at[peer],
            device_id=place(peer),
            device_id_type=MESH,
        )

    def hand_over(peer):
        return pltpu.make_async_remote_copy(
            src_ref=mine.at[peer, pl.ds(0, KV_ROWS)],
            dst_ref=other.at[peer],
            send_sem=pass_send.at[peer],
            recv_sem=pass_recv.at[peer],
            device_id={"half": 1 - side},
            device_id_type=MESH,
        )

    for t in range(quads):
        for load in loads[t]:
            load.wait()
        quad = flip(own_quad, order[t], quads)
        q = dot(x, wq[t]) * (size ** (-0.5) * LOG2E)
        k = dot(x, wk[t])
        v = dot(x, wv[t])
        for i in range(QUAD):
            part = slice(i * size, (i + 1) * size)
            peer = quad * QUAD + i
            sent[peer, 0:MOST, :] = jnp.concatenate([k[:, part], v[:, part]], axis=1).astype(BF16)
            sent[peer, MOST:KV_ROWS, :] = counts
            sent[peer, KV_ROWS:SEND_ROWS, :] = jnp.concatenate(
                [q[0:HALF, part], q[HALF:MOST, part]], axis=1
            ).astype(BF16)
            if order[t] > 0:
                send(peer).start()
            else:

                @pl.when(peer != head)
                def _():
                    send(peer).start()

    mine[head] = sent[head]
    hand_over(head).start()
    for t in range(quads):
        quad = flip(own_quad, order[t], quads)
        for i in range(QUAD):
            peer = quad * QUAD + i
            if order[t] > 0:
                arrival(peer).wait_recv()
                hand_over(peer).start()
            else:

                @pl.when(peer != head)
                def _():
                    arrival(peer).wait_recv()
                    hand_over(peer).start()

    for i in range(1, HEADS):
        send(lax.rem(head + i, HEADS)).wait_send()
    for i in range(HEADS):
        hand_over(i).wait()


def project(mask, gain, volume, wqk, wv):
    tokens, width = volume.shape
    quads = HEADS // QUAD
    cols = width // quads
    lanes = 2 * (width // HEADS)
    whole = pl.BlockSpec(memory_space=pltpu.VMEM)
    dma = pltpu.SemaphoreType.DMA
    return pl.pallas_call(
        project_kernel,
        in_specs=[whole] * 2 + [pl.BlockSpec(memory_space=pl.ANY)] * 3,
        out_specs=[whole] * 3,
        out_shape=[
            jax.ShapeDtypeStruct((MOST, width), BF16),
            jax.ShapeDtypeStruct((HEADS, SEND_ROWS, lanes), BF16),
            jax.ShapeDtypeStruct((HEADS, KV_ROWS, lanes), BF16),
        ],
        scratch_shapes=[
            pltpu.VMEM((tokens, width), BF16),
            pltpu.VMEM((quads, width, cols), BF16),
            pltpu.VMEM((quads, width, cols), BF16),
            pltpu.VMEM((quads, width, cols), BF16),
            pltpu.VMEM((HEADS, SEND_ROWS, lanes), BF16),
            dma((3 * quads + 1,)),
            dma((HEADS,)),
            dma((HEADS,)),
            dma((HEADS,)),
            dma((HEADS,)),
        ],
        compiler_params=pltpu.CompilerParams(
            vmem_limit_bytes=52 << 20, collective_id=0, has_side_effects=True
        ),
        name="project",
    )(mask, gain, volume, wqk, wv)


TILE = 256


def attend_kernel(counts, mine, other, out, packed, queries, keys, values, results):
    blocks = mine.shape[0]
    lanes = mine.shape[2]
    size = lanes // 2
    total = keys.shape[0]
    half = total // 2
    zero = jnp.zeros((MOST, size), F32)
    offset = 0
    starts = []
    for i in range(2 * blocks):
        source = mine if i < blocks else other
        packed[pl.ds(offset, MOST), :] = source[i % blocks, 0:MOST, :].astype(F32)
        if i < blocks:
            starts.append(offset)
        offset = offset + counts[i]
    for i in range(0, total, TILE):
        both = packed[i : i + TILE, :]
        keys[i : i + TILE, :] = both.astype(BF16)
        values[i : i + TILE, :] = jnp.where(iota((TILE, lanes), 1) < size, 1.0, both).astype(BF16)
    for i in range(blocks):
        q = mine[i, KV_ROWS:SEND_ROWS, :].astype(F32)
        q = jnp.concatenate([q[:, :size], q[:, size:]], axis=0)
        packed[pl.ds(starts[i], MOST), :] = jnp.concatenate([q, zero], axis=1)
    for i in range(0, half, TILE):
        queries[i : i + TILE, :] = packed[i : i + TILE, :].astype(BF16)
    results[half:, :] = jnp.zeros((results.shape[0] - half, lanes), F32)

    def step(t, carry):
        at = pl.multiple_of(t * TILE, TILE)
        scores = dot_nt(queries[pl.ds(at, TILE), :], keys[...])
        top = jnp.max(scores, axis=-1, keepdims=True)
        weight = jnp.exp2(scores - top).astype(BF16)
        mixed = dot(weight, values[...])
        results[pl.ds(at, TILE), :] = mixed / pltpu.roll(mixed, size, 1)
        return carry

    lax.fori_loop(0, half // TILE, step, 0)
    for i in range(blocks):
        block = results[pl.ds(starts[i], MOST), :][:, size:]
        out[i, :, :] = jnp.concatenate([block[0:HALF], block[HALF:MOST]], axis=1).astype(BF16)


def attend(counts, mine, other, total):
    blocks, _, lanes = mine.shape
    whole = pl.BlockSpec(memory_space=pltpu.VMEM)
    return pl.pallas_call(
        attend_kernel,
        in_specs=[pl.BlockSpec(memory_space=pltpu.SMEM), whole, whole],
        out_specs=whole,
        out_shape=jax.ShapeDtypeStruct((blocks, HALF, lanes), BF16),
        scratch_shapes=[
            pltpu.VMEM((total + MOST, lanes), F32),
            pltpu.VMEM((total // 2, lanes), BF16),
            pltpu.VMEM((total, lanes), BF16),
            pltpu.VMEM((total, lanes), BF16),
            pltpu.VMEM((total // 2 + MOST, lanes), F32),
        ],
        compiler_params=pltpu.CompilerParams(vmem_limit_bytes=48 << 20),
        name="attend",
    )(counts, mine, other)


def finish_kernel(
    plane_rows,
    context,
    mask,
    rows,
    gain,
    mask_token,
    depth_pos,
    row_pos,
    col_pos,
    dec_gain,
    wo_hbm,
    embed_hbm,
    wqk_hbm,
    wv_hbm,
    dec_wo_hbm,
    out,
    wo,
    embed,
    wqk,
    wv,
    dec_wo,
    landed,
    streams,
    columns,
    queries,
    keys,
    values,
    decoded,
    load_sem,
    head_send,
    head_recv,
    part_send,
    part_recv,
    back_send,
    back_recv,
):
    slab, y = lax.axis_index("slab"), lax.axis_index("y")
    y_count, slab_count = lax.axis_size("y"), lax.axis_size("slab")
    heads, _, lanes = context.shape
    depth, spots, dec_width = out.shape
    tokens = depth * spots
    plane_cols = tokens // plane_rows
    head = slab * y_count + y
    level = lax.axis_index("win") * slab_count + slab
    size = lanes // 2

    loads = []
    for i, (source, target) in enumerate(
        ((wo_hbm, wo), (embed_hbm, embed), (wqk_hbm, wqk), (wv_hbm, wv), (dec_wo_hbm, dec_wo))
    ):
        load = pltpu.make_async_copy(source, target, load_sem.at[i])
        load.start()
        loads.append(load)

    def head_device(i):
        peer = flip(head, heads - i, heads)
        return peer, {"slab": peer // y_count, "y": lax.rem(peer, y_count)}

    def level_device(i):
        peer = flip(level, depth - i, depth)
        return peer, {"win": peer // slab_count, "slab": lax.rem(peer, slab_count)}

    barrier = pltpu.get_barrier_semaphore()
    for i in range(1, heads):
        _, place = head_device(i)
        pl.semaphore_signal(barrier, inc=1, device_id=place, device_id_type=MESH)
    for i in range(1, depth):
        _, place = level_device(i)
        pl.semaphore_signal(barrier, inc=1, device_id=place, device_id_type=MESH)
    pl.semaphore_wait(barrier, heads + depth - 2)

    head_copies = []
    for i in range(1, heads):
        peer, place = head_device(i)
        copy = pltpu.make_async_remote_copy(
            src_ref=context.at[peer],
            dst_ref=landed.at[head],
            send_sem=head_send.at[i],
            recv_sem=head_recv.at[i],
            device_id=place,
            device_id_type=MESH,
        )
        copy.start()
        head_copies.append(copy)
    landed[head] = context[head]

    seen = jnp.where(mask_row(mask) == 1, 1.0, 0.0)
    seen = jnp.broadcast_to(seen, (16, tokens)).astype(BF16)
    down, across = iota((tokens, tokens), 0), iota((tokens, tokens), 1)
    rank = dot_nt(jnp.where(across <= down, 1.0, 0.0).astype(BF16), seen)[:, 0:1]
    shown = dot_nt(jnp.where(across == down, 1.0, 0.0).astype(BF16), seen)[:, 0:1] > 0.5
    rank = jnp.where(shown, rank.astype(jnp.int32) - 1, -1)
    place = jnp.where(iota((tokens, MOST), 1) == rank, 1.0, 0.0).astype(BF16)
    grp = y * lax.axis_size("half") + lax.axis_index("half")
    depths = depth_pos[...].astype(F32)
    chosen = jnp.where(iota(depths.shape, 0) == level, depths, 0.0)
    chosen = jnp.sum(chosen, axis=0, keepdims=True)
    row_count, col_count = row_pos.shape[0], col_pos.shape[0]
    row = iota((tokens, row_count), 0) // plane_cols + grp * plane_rows
    row_hot = jnp.where(iota((tokens, row_count), 1) == row, 1.0, 0.0).astype(BF16)
    row_part = dot(row_hot, row_pos[...])
    col = iota((tokens, col_count), 0) % plane_cols
    col_hot = jnp.where(iota((tokens, col_count), 1) == col, 1.0, 0.0).astype(BF16)
    col_part = dot(col_hot, col_pos[...])

    loads[0].wait()
    loads[1].wait()
    for copy in head_copies:
        copy.wait()
    tiles = []
    for j in range(0, heads, 2):
        a, b = landed[j], landed[j + 1]
        tiles.append(
            jnp.concatenate(
                [
                    jnp.concatenate([a[:, :size], b[:, :size]], axis=1),
                    jnp.concatenate([a[:, size:], b[:, size:]], axis=1),
                ],
                axis=0,
            )
        )
    mixed = rows[...].astype(F32) + dot(jnp.concatenate(tiles, axis=1), wo[...])
    encoded = norm(mixed, gain[...]).astype(BF16)
    embedded = dot(encoded, embed[...]).astype(BF16)
    stream = dot(place, embedded)
    stream = jnp.where(shown, stream, mask_token[...].astype(F32))
    stream = ((stream + chosen) + row_part) + col_part
    streams[...] = stream.reshape(depth, spots, dec_width).astype(BF16)

    def part_copy(i):
        peer, where = level_device(i)
        return pltpu.make_async_remote_copy(
            src_ref=streams.at[peer],
            dst_ref=columns.at[level],
            send_sem=part_send.at[i],
            recv_sem=part_recv.at[i],
            device_id=where,
            device_id_type=MESH,
        )

    def back_copy(i):
        peer, where = level_device(i)
        return pltpu.make_async_remote_copy(
            src_ref=decoded.at[peer],
            dst_ref=out.at[level],
            send_sem=back_send.at[i],
            recv_sem=back_recv.at[i],
            device_id=where,
            device_id_type=MESH,
        )

    def start_part(i, carry):
        part_copy(i).start()
        return carry

    lax.fori_loop(1, depth, start_part, 0)
    columns[level] = streams[level]
    for load in loads[2:]:
        load.wait()

    def wait_part(i, carry):
        part_copy(i).wait()
        return carry

    lax.fori_loop(1, depth, wait_part, 0)
    x = columns[...].astype(F32).reshape(tokens, dec_width)
    normed = norm(x, dec_gain[...]).astype(BF16)
    shape = (depth, spots, dec_width)
    queries[...] = dot(normed, wqk[:, :dec_width]).astype(BF16).astype(F32).reshape(shape)
    keys[...] = dot(normed, wqk[:, dec_width:]).astype(BF16).astype(F32).reshape(shape)
    values[...] = dot(normed, wv[...]).astype(BF16).astype(F32).reshape(shape)
    dec_size = dec_width // DHEADS
    wide = 128
    gather = jnp.where(
        iota((dec_width, wide), 0) // dec_size == iota((dec_width, wide), 1), 1.0, 0.0
    ).astype(BF16)
    spread = jnp.where(
        iota((wide, dec_width), 1) // dec_size == iota((wide, dec_width), 0), 1.0, 0.0
    ).astype(BF16)

    def decode(z):
        product = (keys[...] * queries[z][None]).reshape(tokens, dec_width)
        scores = dot(product.astype(BF16), gather) * dec_size ** (-0.5)
        scores = scores.reshape(depth, spots, wide)
        exponent = jnp.exp(scores - jnp.max(scores, axis=0, keepdims=True))
        probs = exponent / jnp.sum(exponent, axis=0, keepdims=True)
        probs = dot(probs.reshape(tokens, wide).astype(BF16), spread).reshape(shape)
        result = jnp.sum(probs * values[...], axis=0).astype(BF16)
        return (columns[z].astype(F32) + dot(result, dec_wo[...])).astype(BF16)

    def step(i, carry):
        z = flip(level, depth - i, depth)
        decoded[z] = decode(z)
        back_copy(i).start()
        return carry

    lax.fori_loop(1, depth, step, 0)
    out[level] = decode(level)

    def wait_back(i, carry):
        back_copy(i).wait()
        return carry

    lax.fori_loop(1, depth, wait_back, 0)


def finish(plane_rows, depth, context, mask, rows, *others):
    tokens = mask.shape[1] * mask.shape[2]
    weights = others[-5:]
    dec_width = weights[1].shape[1]
    heads = context.shape[0]
    whole = pl.BlockSpec(memory_space=pltpu.VMEM)
    shape = (depth, tokens // depth, dec_width)
    dma = pltpu.SemaphoreType.DMA
    return pl.pallas_call(
        functools.partial(finish_kernel, plane_rows),
        in_specs=[whole] * 9 + [pl.BlockSpec(memory_space=pl.ANY)] * 5,
        out_specs=whole,
        out_shape=jax.ShapeDtypeStruct(shape, BF16),
        scratch_shapes=[pltpu.VMEM(w.shape, BF16) for w in weights]
        + [
            pltpu.VMEM(context.shape, BF16),
            pltpu.VMEM(shape, BF16),
            pltpu.VMEM(shape, BF16),
            pltpu.VMEM(shape, F32),
            pltpu.VMEM(shape, F32),
            pltpu.VMEM(shape, F32),
            pltpu.VMEM(shape, BF16),
            dma((5,)),
            dma((heads,)),
            dma((heads,)),
            dma((depth,)),
            dma((depth,)),
            dma((depth,)),
            dma((depth,)),
        ],
        compiler_params=pltpu.CompilerParams(
            vmem_limit_bytes=48 << 20, collective_id=1, has_side_effects=True
        ),
        name="finish",
    )(context, mask, rows, *others)


def per_device(
    volume,
    vis_mask,
    enc_gain,
    enc_wqk,
    enc_wv,
    enc_wo,
    final_gain,
    embed_w,
    mask_token,
    depth_pos,
    row_pos,
    col_pos,
    dec_gain,
    dec_wqk,
    dec_wv,
    dec_wo,
):
    _, plane_rows, plane_cols, width = volume.shape
    tokens = plane_rows * plane_cols
    rows, mine, other = project(
        vis_mask, enc_gain, volume.reshape(tokens, width), enc_wqk, enc_wv
    )
    counts = jnp.concatenate([mine[:, MOST, 0], other[:, MOST, 0]]).astype(jnp.int32)
    window_tokens = WIN_SLABS * tokens * lax.axis_size("y") * lax.axis_size("half")
    context = attend(counts, mine, other, window_tokens // 4)
    decoded = finish(
        plane_rows,
        depth_pos.shape[0],
        context,
        vis_mask,
        rows,
        final_gain.reshape(1, width),
        mask_token.reshape(1, -1),
        depth_pos,
        row_pos,
        col_pos,
        dec_gain.reshape(1, -1),
        enc_wo,
        embed_w,
        dec_wqk,
        dec_wv,
        dec_wo,
    )
    return decoded.reshape(1, plane_rows, plane_cols, -1)


def solution(mesh):
    slabs, groups = mesh.devices.shape
    split = Mesh(
        mesh.devices.reshape(slabs // WIN_SLABS, WIN_SLABS, groups // 2, 2),
        ("win", "slab", "y", "half"),
    )
    placed = (
        P(("win", "slab"), ("y", "half"), None, None),
        P(("win", "slab"), ("y", "half"), None),
    ) + (P(),) * 14
    return jax.shard_map(
        per_device,
        mesh=split,
        in_specs=placed,
        out_specs=P(("win", "slab"), ("y", "half"), None, None),
        check_vma=False,
    )
```

```python
import functools

import jax
import jax.numpy as jnp
from jax import lax
from jax.experimental import pallas as pl
from jax.experimental.pallas import tpu as pltpu
from jax.sharding import Mesh, PartitionSpec as P

HEADS = 16
DHEADS = 16
WIN_SLABS = 8
MOST = 192
HALF = MOST // 2
COUNT_ROWS = 16
KV_ROWS = MOST + COUNT_ROWS
SEND_ROWS = KV_ROWS + HALF
QUAD = 4
LOG2E = 1.4426950408889634
F32 = jnp.float32
BF16 = jnp.bfloat16
MESH = pl.DeviceIdType.MESH


def dot(a, b):
    return lax.dot_general(a, b, (((1,), (0,)), ((), ())), preferred_element_type=F32)


def dot_nt(a, b):
    return lax.dot_general(a, b, (((1,), (1,)), ((), ())), preferred_element_type=F32)


def norm(values, gain):
    average = jnp.mean(values, axis=-1, keepdims=True)
    centered = values - average
    variance = jnp.mean(centered * centered, axis=-1, keepdims=True)
    return centered * lax.rsqrt(variance + 1e-05) * gain.astype(F32)


def iota(shape, dim):
    return lax.broadcasted_iota(jnp.int32, shape, dim)


def flip(position, bits, count):
    result, weight = 0, 1
    while weight < count:
        result = result + lax.rem(position // weight + bits // weight, 2) * weight
        weight *= 2
    return result


def mask_row(mask):
    return jnp.concatenate([mask[0, r : r + 1, :] for r in range(mask.shape[1])], axis=1)


def project_kernel(
    mask,
    gain,
    volume_hbm,
    wqk_hbm,
    wv_hbm,
    rows,
    mine,
    other,
    volume,
    wq,
    wk,
    wv,
    sent,
    load_sem,
    send_sem,
    recv_sem,
    pass_send,
    pass_recv,
):
    slab, y, side = lax.axis_index("slab"), lax.axis_index("y"), lax.axis_index("half")
    y_count = lax.axis_size("y")
    tokens, width = volume.shape
    quads, _, cols = wq.shape
    head = slab * y_count + y
    own_quad = head // QUAD
    order = [quads // 2 + t for t in range(quads // 2)] + list(range(quads // 2 - 1, -1, -1))

    first = pltpu.make_async_copy(volume_hbm, volume, load_sem.at[3 * quads])
    first.start()
    loads = []
    for t in range(quads):
        quad = flip(own_quad, order[t], quads)
        at = pl.multiple_of(quad * cols, cols)
        group = [
            pltpu.make_async_copy(
                wqk_hbm.at[:, pl.ds(at, cols)], wq.at[t], load_sem.at[3 * t]
            ),
            pltpu.make_async_copy(
                wqk_hbm.at[:, pl.ds(at + width, cols)], wk.at[t], load_sem.at[3 * t + 1]
            ),
            pltpu.make_async_copy(
                wv_hbm.at[:, pl.ds(at, cols)], wv.at[t], load_sem.at[3 * t + 2]
            ),
        ]
        for load in group:
            load.start()
        loads.append(group)

    def place(peer):
        return {"slab": peer // y_count, "y": lax.rem(peer, y_count)}

    barrier = pltpu.get_barrier_semaphore()
    for i in range(1, HEADS):
        peer = lax.rem(head + i, HEADS)
        pl.semaphore_signal(barrier, inc=1, device_id=place(peer), device_id_type=MESH)
    pl.semaphore_signal(barrier, inc=1, device_id={"half": 1 - side}, device_id_type=MESH)

    seen = mask_row(mask) == 1
    count = jnp.sum(jnp.where(seen, 1.0, 0.0), axis=1, keepdims=True)
    seen_rows = jnp.broadcast_to(jnp.where(seen, 1.0, 0.0), (16, tokens)).astype(BF16)
    upper = jnp.where(iota((tokens, tokens), 0) <= iota((tokens, tokens), 1), 1.0, 0.0)
    rank = dot(seen_rows, upper.astype(BF16))[0:1, :].astype(jnp.int32) - 1
    rank = jnp.where(seen, rank, -1)
    pick = jnp.where(iota((MOST, tokens), 0) == rank, 1.0, 0.0).astype(BF16)
    first.wait()
    row_data = dot(pick, volume[...])
    rows[...] = row_data.astype(BF16)
    x = norm(row_data, gain[...].astype(F32).reshape(1, width)).astype(BF16)
    size = cols // QUAD
    counts = jnp.broadcast_to(count, (COUNT_ROWS, 2 * size)).astype(BF16)
    pl.semaphore_wait(barrier, HEADS)

    def send(peer):
        return pltpu.make_async_remote_copy(
            src_ref=sent.at[peer],
            dst_ref=mine.at[head],
            send_sem=send_sem.at[peer],
            recv_sem=recv_sem.at[head],
            device_id=place(peer),
            device_id_type=MESH,
        )

    def arrival(peer):
        return pltpu.make_async_remote_copy(
            src_ref=sent.at[peer],
            dst_ref=mine.at[peer],
            send_sem=send_sem.at[peer],
            recv_sem=recv_sem.at[peer],
            device_id=place(peer),
            device_id_type=MESH,
        )

    def hand_over(peer):
        return pltpu.make_async_remote_copy(
            src_ref=mine.at[peer, pl.ds(0, KV_ROWS)],
            dst_ref=other.at[peer],
            send_sem=pass_send.at[peer],
            recv_sem=pass_recv.at[peer],
            device_id={"half": 1 - side},
            device_id_type=MESH,
        )

    for t in range(quads):
        for load in loads[t]:
            load.wait()
        quad = flip(own_quad, order[t], quads)
        q = dot(x, wq[t]) * (size ** (-0.5) * LOG2E)
        k = dot(x, wk[t])
        v = dot(x, wv[t])
        for i in range(QUAD):
            part = slice(i * size, (i + 1) * size)
            peer = quad * QUAD + i
            sent[peer, 0:MOST, :] = jnp.concatenate([k[:, part], v[:, part]], axis=1).astype(BF16)
            sent[peer, MOST:KV_ROWS, :] = counts
            sent[peer, KV_ROWS:SEND_ROWS, :] = jnp.concatenate(
                [q[0:HALF, part], q[HALF:MOST, part]], axis=1
            ).astype(BF16)
            if order[t] > 0:
                send(peer).start()
            else:

                @pl.when(peer != head)
                def _():
                    send(peer).start()

    mine[head] = sent[head]
    hand_over(head).start()
    for t in range(quads):
        quad = flip(own_quad, order[t], quads)
        for i in range(QUAD):
            peer = quad * QUAD + i
            if order[t] > 0:
                arrival(peer).wait_recv()
                hand_over(peer).start()
            else:

                @pl.when(peer != head)
                def _():
                    arrival(peer).wait_recv()
                    hand_over(peer).start()

    for i in range(1, HEADS):
        send(lax.rem(head + i, HEADS)).wait_send()
    for i in range(HEADS):
        hand_over(i).wait()


def project(mask, gain, volume, wqk, wv):
    tokens, width = volume.shape
    quads = HEADS // QUAD
    cols = width // quads
    lanes = 2 * (width // HEADS)
    whole = pl.BlockSpec(memory_space=pltpu.VMEM)
    dma = pltpu.SemaphoreType.DMA
    return pl.pallas_call(
        project_kernel,
        in_specs=[whole] * 2 + [pl.BlockSpec(memory_space=pl.ANY)] * 3,
        out_specs=[whole] * 3,
        out_shape=[
            jax.ShapeDtypeStruct((MOST, width), BF16),
            jax.ShapeDtypeStruct((HEADS, SEND_ROWS, lanes), BF16),
            jax.ShapeDtypeStruct((HEADS, KV_ROWS, lanes), BF16),
        ],
        scratch_shapes=[
            pltpu.VMEM((tokens, width), BF16),
            pltpu.VMEM((quads, width, cols), BF16),
            pltpu.VMEM((quads, width, cols), BF16),
            pltpu.VMEM((quads, width, cols), BF16),
            pltpu.VMEM((HEADS, SEND_ROWS, lanes), BF16),
            dma((3 * quads + 1,)),
            dma((HEADS,)),
            dma((HEADS,)),
            dma((HEADS,)),
            dma((HEADS,)),
        ],
        compiler_params=pltpu.CompilerParams(
            vmem_limit_bytes=52 << 20, collective_id=0, has_side_effects=True
        ),
        name="project",
    )(mask, gain, volume, wqk, wv)


TILE = 256


def attend_kernel(counts, mine, other, out, packed, queries, keys, values, results):
    blocks = mine.shape[0]
    lanes = mine.shape[2]
    size = lanes // 2
    total = keys.shape[0]
    half = total // 2
    zero = jnp.zeros((MOST, size), F32)
    offset = 0
    starts = []
    for i in range(2 * blocks):
        source = mine if i < blocks else other
        packed[pl.ds(offset, MOST), :] = source[i % blocks, 0:MOST, :].astype(F32)
        if i < blocks:
            starts.append(offset)
        offset = offset + counts[i]
    for i in range(0, total, TILE):
        both = packed[i : i + TILE, :]
        keys[i : i + TILE, :] = both.astype(BF16)
        values[i : i + TILE, :] = jnp.where(iota((TILE, lanes), 1) < size, 1.0, both).astype(BF16)
    for i in range(blocks):
        q = mine[i, KV_ROWS:SEND_ROWS, :].astype(F32)
        q = jnp.concatenate([q[:, :size], q[:, size:]], axis=0)
        packed[pl.ds(starts[i], MOST), :] = jnp.concatenate([q, zero], axis=1)
    for i in range(0, half, TILE):
        queries[i : i + TILE, :] = packed[i : i + TILE, :].astype(BF16)
    results[half:, :] = jnp.zeros((results.shape[0] - half, lanes), F32)

    def step(t, carry):
        at = pl.multiple_of(t * TILE, TILE)
        scores = dot_nt(queries[pl.ds(at, TILE), :], keys[...])
        top = jnp.max(scores, axis=-1, keepdims=True)
        weight = jnp.exp2(scores - top).astype(BF16)
        mixed = dot(weight, values[...])
        results[pl.ds(at, TILE), :] = mixed / pltpu.roll(mixed, size, 1)
        return carry

    lax.fori_loop(0, half // TILE, step, 0, unroll=2)
    for i in range(blocks):
        block = results[pl.ds(starts[i], MOST), :][:, size:]
        out[i, :, :] = jnp.concatenate([block[0:HALF], block[HALF:MOST]], axis=1).astype(BF16)


def attend(counts, mine, other, total):
    blocks, _, lanes = mine.shape
    whole = pl.BlockSpec(memory_space=pltpu.VMEM)
    return pl.pallas_call(
        attend_kernel,
        in_specs=[pl.BlockSpec(memory_space=pltpu.SMEM), whole, whole],
        out_specs=whole,
        out_shape=jax.ShapeDtypeStruct((blocks, HALF, lanes), BF16),
        scratch_shapes=[
            pltpu.VMEM((total + MOST, lanes), F32),
            pltpu.VMEM((total // 2, lanes), BF16),
            pltpu.VMEM((total, lanes), BF16),
            pltpu.VMEM((total, lanes), BF16),
            pltpu.VMEM((total // 2 + MOST, lanes), F32),
        ],
        compiler_params=pltpu.CompilerParams(vmem_limit_bytes=48 << 20),
        name="attend",
    )(counts, mine, other)


def finish_kernel(
    plane_rows,
    context,
    mask,
    rows,
    gain,
    mask_token,
    depth_pos,
    row_pos,
    col_pos,
    dec_gain,
    wo_hbm,
    embed_hbm,
    wqk_hbm,
    wv_hbm,
    dec_wo_hbm,
    out,
    wo,
    embed,
    wqk,
    wv,
    dec_wo,
    landed,
    streams,
    columns,
    queries,
    keys,
    values,
    decoded,
    load_sem,
    head_send,
    head_recv,
    part_send,
    part_recv,
    back_send,
    back_recv,
):
    slab, y = lax.axis_index("slab"), lax.axis_index("y")
    y_count, slab_count = lax.axis_size("y"), lax.axis_size("slab")
    heads, _, lanes = context.shape
    depth, spots, dec_width = out.shape
    tokens = depth * spots
    plane_cols = tokens // plane_rows
    head = slab * y_count + y
    level = lax.axis_index("win") * slab_count + slab
    size = lanes // 2

    loads = []
    for i, (source, target) in enumerate(
        ((wo_hbm, wo), (embed_hbm, embed), (wqk_hbm, wqk), (wv_hbm, wv), (dec_wo_hbm, dec_wo))
    ):
        load = pltpu.make_async_copy(source, target, load_sem.at[i])
        load.start()
        loads.append(load)

    def head_device(i):
        peer = flip(head, heads - i, heads)
        return peer, {"slab": peer // y_count, "y": lax.rem(peer, y_count)}

    def level_device(i):
        peer = flip(level, depth - i, depth)
        return peer, {"win": peer // slab_count, "slab": lax.rem(peer, slab_count)}

    barrier = pltpu.get_barrier_semaphore()
    for i in range(1, heads):
        _, place = head_device(i)
        pl.semaphore_signal(barrier, inc=1, device_id=place, device_id_type=MESH)
    for i in range(1, depth):
        _, place = level_device(i)
        pl.semaphore_signal(barrier, inc=1, device_id=place, device_id_type=MESH)
    pl.semaphore_wait(barrier, heads + depth - 2)

    head_copies = []
    for i in range(1, heads):
        peer, place = head_device(i)
        copy = pltpu.make_async_remote_copy(
            src_ref=context.at[peer],
            dst_ref=landed.at[head],
            send_sem=head_send.at[i],
            recv_sem=head_recv.at[i],
            device_id=place,
            device_id_type=MESH,
        )
        copy.start()
        head_copies.append(copy)
    landed[head] = context[head]

    seen = jnp.where(mask_row(mask) == 1, 1.0, 0.0)
    seen = jnp.broadcast_to(seen, (16, tokens)).astype(BF16)
    down, across = iota((tokens, tokens), 0), iota((tokens, tokens), 1)
    rank = dot_nt(jnp.where(across <= down, 1.0, 0.0).astype(BF16), seen)[:, 0:1]
    shown = dot_nt(jnp.where(across == down, 1.0, 0.0).astype(BF16), seen)[:, 0:1] > 0.5
    rank = jnp.where(shown, rank.astype(jnp.int32) - 1, -1)
    place = jnp.where(iota((tokens, MOST), 1) == rank, 1.0, 0.0).astype(BF16)
    grp = y * lax.axis_size("half") + lax.axis_index("half")
    depths = depth_pos[...].astype(F32)
    chosen = jnp.where(iota(depths.shape, 0) == level, depths, 0.0)
    chosen = jnp.sum(chosen, axis=0, keepdims=True)
    row_count, col_count = row_pos.shape[0], col_pos.shape[0]
    row = iota((tokens, row_count), 0) // plane_cols + grp * plane_rows
    row_hot = jnp.where(iota((tokens, row_count), 1) == row, 1.0, 0.0).astype(BF16)
    row_part = dot(row_hot, row_pos[...])
    col = iota((tokens, col_count), 0) % plane_cols
    col_hot = jnp.where(iota((tokens, col_count), 1) == col, 1.0, 0.0).astype(BF16)
    col_part = dot(col_hot, col_pos[...])

    loads[0].wait()
    loads[1].wait()
    for copy in head_copies:
        copy.wait()
    tiles = []
    for j in range(0, heads, 2):
        a, b = landed[j], landed[j + 1]
        tiles.append(
            jnp.concatenate(
                [
                    jnp.concatenate([a[:, :size], b[:, :size]], axis=1),
                    jnp.concatenate([a[:, size:], b[:, size:]], axis=1),
                ],
                axis=0,
            )
        )
    mixed = rows[...].astype(F32) + dot(jnp.concatenate(tiles, axis=1), wo[...])
    encoded = norm(mixed, gain[...]).astype(BF16)
    embedded = dot(encoded, embed[...]).astype(BF16)
    stream = dot(place, embedded)
    stream = jnp.where(shown, stream, mask_token[...].astype(F32))
    stream = ((stream + chosen) + row_part) + col_part
    streams[...] = stream.reshape(depth, spots, dec_width).astype(BF16)

    def part_copy(i):
        peer, where = level_device(i)
        return pltpu.make_async_remote_copy(
            src_ref=streams.at[peer],
            dst_ref=columns.at[level],
            send_sem=part_send.at[i],
            recv_sem=part_recv.at[i],
            device_id=where,
            device_id_type=MESH,
        )

    def back_copy(i):
        peer, where = level_device(i)
        return pltpu.make_async_remote_copy(
            src_ref=decoded.at[peer],
            dst_ref=out.at[level],
            send_sem=back_send.at[i],
            recv_sem=back_recv.at[i],
            device_id=where,
            device_id_type=MESH,
        )

    def start_part(i, carry):
        part_copy(i).start()
        return carry

    lax.fori_loop(1, depth, start_part, 0)
    columns[level] = streams[level]
    for load in loads[2:]:
        load.wait()

    def wait_part(i, carry):
        part_copy(i).wait()
        return carry

    lax.fori_loop(1, depth, wait_part, 0)
    x = columns[...].astype(F32).reshape(tokens, dec_width)
    normed = norm(x, dec_gain[...]).astype(BF16)
    shape = (depth, spots, dec_width)
    queries[...] = dot(normed, wqk[:, :dec_width]).astype(BF16).astype(F32).reshape(shape)
    keys[...] = dot(normed, wqk[:, dec_width:]).astype(BF16).astype(F32).reshape(shape)
    values[...] = dot(normed, wv[...]).astype(BF16).astype(F32).reshape(shape)
    dec_size = dec_width // DHEADS
    wide = 128
    gather = jnp.where(
        iota((dec_width, wide), 0) // dec_size == iota((dec_width, wide), 1), 1.0, 0.0
    ).astype(BF16)
    spread = jnp.where(
        iota((wide, dec_width), 1) // dec_size == iota((wide, dec_width), 0), 1.0, 0.0
    ).astype(BF16)

    def decode(z):
        product = (keys[...] * queries[z][None]).reshape(tokens, dec_width)
        scores = dot(product.astype(BF16), gather) * dec_size ** (-0.5)
        scores = scores.reshape(depth, spots, wide)
        exponent = jnp.exp(scores - jnp.max(scores, axis=0, keepdims=True))
        probs = exponent / jnp.sum(exponent, axis=0, keepdims=True)
        probs = dot(probs.reshape(tokens, wide).astype(BF16), spread).reshape(shape)
        result = jnp.sum(probs * values[...], axis=0).astype(BF16)
        return (columns[z].astype(F32) + dot(result, dec_wo[...])).astype(BF16)

    def step(i, carry):
        z = flip(level, depth - i, depth)
        decoded[z] = decode(z)
        back_copy(i).start()
        return carry

    lax.fori_loop(1, depth, step, 0)
    out[level] = decode(level)

    def wait_back(i, carry):
        back_copy(i).wait()
        return carry

    lax.fori_loop(1, depth, wait_back, 0)


def finish(plane_rows, depth, context, mask, rows, *others):
    tokens = mask.shape[1] * mask.shape[2]
    weights = others[-5:]
    dec_width = weights[1].shape[1]
    heads = context.shape[0]
    whole = pl.BlockSpec(memory_space=pltpu.VMEM)
    shape = (depth, tokens // depth, dec_width)
    dma = pltpu.SemaphoreType.DMA
    return pl.pallas_call(
        functools.partial(finish_kernel, plane_rows),
        in_specs=[whole] * 9 + [pl.BlockSpec(memory_space=pl.ANY)] * 5,
        out_specs=whole,
        out_shape=jax.ShapeDtypeStruct(shape, BF16),
        scratch_shapes=[pltpu.VMEM(w.shape, BF16) for w in weights]
        + [
            pltpu.VMEM(context.shape, BF16),
            pltpu.VMEM(shape, BF16),
            pltpu.VMEM(shape, BF16),
            pltpu.VMEM(shape, F32),
            pltpu.VMEM(shape, F32),
            pltpu.VMEM(shape, F32),
            pltpu.VMEM(shape, BF16),
            dma((5,)),
            dma((heads,)),
            dma((heads,)),
            dma((depth,)),
            dma((depth,)),
            dma((depth,)),
            dma((depth,)),
        ],
        compiler_params=pltpu.CompilerParams(
            vmem_limit_bytes=48 << 20, collective_id=1, has_side_effects=True
        ),
        name="finish",
    )(context, mask, rows, *others)


def per_device(
    volume,
    vis_mask,
    enc_gain,
    enc_wqk,
    enc_wv,
    enc_wo,
    final_gain,
    embed_w,
    mask_token,
    depth_pos,
    row_pos,
    col_pos,
    dec_gain,
    dec_wqk,
    dec_wv,
    dec_wo,
):
    _, plane_rows, plane_cols, width = volume.shape
    tokens = plane_rows * plane_cols
    rows, mine, other = project(
        vis_mask, enc_gain, volume.reshape(tokens, width), enc_wqk, enc_wv
    )
    counts = jnp.concatenate([mine[:, MOST, 0], other[:, MOST, 0]]).astype(jnp.int32)
    window_tokens = WIN_SLABS * tokens * lax.axis_size("y") * lax.axis_size("half")
    context = attend(counts, mine, other, window_tokens // 4)
    decoded = finish(
        plane_rows,
        depth_pos.shape[0],
        context,
        vis_mask,
        rows,
        final_gain.reshape(1, width),
        mask_token.reshape(1, -1),
        depth_pos,
        row_pos,
        col_pos,
        dec_gain.reshape(1, -1),
        enc_wo,
        embed_w,
        dec_wqk,
        dec_wv,
        dec_wo,
    )
    return decoded.reshape(1, plane_rows, plane_cols, -1)


def solution(mesh):
    slabs, groups = mesh.devices.shape
    split = Mesh(
        mesh.devices.reshape(slabs // WIN_SLABS, WIN_SLABS, groups // 2, 2),
        ("win", "slab", "y", "half"),
    )
    placed = (
        P(("win", "slab"), ("y", "half"), None, None),
        P(("win", "slab"), ("y", "half"), None),
    ) + (P(),) * 14
    return jax.shard_map(
        per_device,
        mesh=split,
        in_specs=placed,
        out_specs=P(("win", "slab"), ("y", "half"), None, None),
        check_vma=False,
    )
```
